512 devices in a mesh: dp: 32 (over z, core), mp: 16 (over y, x).
Axes of the slice: x: 4, y: 4, z: 16, core: 2. Of those that a mesh axis runs over, the one named last changes fastest.
Arguments:
- grad: bfloat16 [32, 512, 6144], P(None, 'dp', 'mp'), may hold values from -100 to 100
- momentum: float32 [32, 512, 6144], P(None, 'dp', 'mp'), may hold values from -200 to 200
- old_slot: int32 [32], replicated, may hold values from 0 to 31, each once
- new_slot: int32 [32], replicated, may hold values from 0 to 31, each once
Outputs:
- new_momentum: float32 [32, 512, 6144], P(None, 'dp', 'mp')
- update: bfloat16 [32, 512, 6144], P(None, 'dp', 'mp')
The draws below stay inside these ranges and needn't reach their ends.
Inputs may be any that keep to these rules, and one draw needn't show every extreme that they name: old_slot and new_slot are each a permutation of the matrices. `new_slot`: a permutation.
All inputs are finite; a program needn't handle non-finite values.
Results may differ from the reference program's by a relative error of at most 0.0053.
Values may be sent and summed in bfloat16 or wider, within the bound.
No kernel may reach another device: no remote copies, remote signals or barrier semaphores. Data moves between devices by JAX's collectives and lax.ppermute only.
A program may use at most 64 MiB of HBM per device.

```python
import math
import jax
import jax.numpy as jnp
from jax import lax

KV_RANK = 512
ITERS = 3
KEY_COLS = 6144
NMAT = 32
N_MP = 16


def scale_field(key, noise, row_span, amplitude):
    k_rows, k_cols, k_mats = jax.random.split(key, 3)
    rows = jnp.exp(jax.random.uniform(k_rows, (NMAT, KV_RANK, 1), jnp.float32, -row_span, row_span))
    cols = jnp.exp(jax.random.uniform(k_cols, (1, 1, KEY_COLS), jnp.float32, -1.15, 1.15))
    ramp = 0.5 + jnp.arange(KEY_COLS, dtype=jnp.float32)[None, None, :] / KEY_COLS
    mats = jnp.exp(jax.random.uniform(k_mats, (NMAT, 1, 1), jnp.float32, -0.7, 0.7))
    return amplitude * noise * rows * cols * ramp * mats


def draw_grad(key, part):
    key = jax.random.fold_in(key, 5)
    k_noise, k_rest = jax.random.split(key)
    noise = jax.random.truncated_normal(k_noise, -4.0, 4.0, (NMAT, KV_RANK, KEY_COLS), jnp.float32)
    return scale_field(k_rest, noise, 1.15, 0.5).astype(jnp.bfloat16)


def draw_momentum(key, part):
    key = jax.random.fold_in(key, 9)
    k_noise, k_rest = jax.random.split(key)
    noise = jax.random.truncated_normal(k_noise, -4.0, 4.0, (NMAT, KV_RANK, KEY_COLS), jnp.float32)
    return scale_field(k_rest, noise, 1.15, 1.0)


def setup_inputs(seed: int = 0) -> dict:
    key_list = jax.random.split(jax.random.key(seed), 5)
    grad = draw_grad(jax.random.fold_in(key_list[4], 71), 0)
    momentum = draw_momentum(jax.random.fold_in(key_list[4], 71), 0)
    old_slot = jax.random.permutation(key_list[2], NMAT).astype(jnp.int32)
    new_slot = jax.random.permutation(key_list[3], NMAT).astype(jnp.int32)
    return {"grad": grad, "momentum": momentum, "old_slot": old_slot, "new_slot": new_slot}


coef_a = 3.4445
coef_b = -4.775
coef_c = 2.0315
beta = 0.95
epsilon = 1e-07

def polish(merged):
    start = merged.astype(jnp.bfloat16)
    start_wide = start.astype(jnp.float32)
    total = jnp.sum(start_wide * start_wide)
    current = start_wide / (jnp.sqrt(total) + epsilon)
    width = merged.shape[1]
    for step in range(ITERS):
        pieces = current.reshape(merged.shape[0], N_MP, width // N_MP)
        partial_value = jnp.einsum('rkc,skc->krs', pieces, pieces, precision=lax.Precision.HIGHEST)
        gram = lax.optimization_barrier(jnp.sum(partial_value, axis=0))
        square = jnp.dot(gram, gram, precision=lax.Precision.HIGHEST, preferred_element_type=jnp.float32)
        poly = coef_b * gram + coef_c * square
        current = coef_a * current + jnp.dot(poly, current, precision=lax.Precision.HIGHEST, preferred_element_type=jnp.float32)
    return (0.2 * math.sqrt(width) * current).astype(jnp.bfloat16)

def reference(grad, momentum, old_slot, new_slot):
    count = new_slot.shape[0]
    mom_by = jnp.take(momentum, old_slot.astype(jnp.int32), axis=0)
    grad_by = jnp.take(grad, new_slot.astype(jnp.int32), axis=0)
    merged = beta * mom_by + grad_by.astype(jnp.float32)
    updates = lax.map(polish, merged)
    placing = jnp.zeros((count,), jnp.int32).at[new_slot.astype(jnp.int32)].set(jnp.arange(count, dtype=jnp.int32))
    return (jnp.take(merged, placing, axis=0), jnp.take(updates, placing, axis=0))
```

```python
import math

import jax
import jax.numpy as jnp
from jax import lax
from jax.experimental import pallas as pl
from jax.experimental.pallas import tpu as pltpu
from jax.sharding import PartitionSpec as P

coef_a = 3.4445
coef_b = -4.775
coef_c = 2.0315
beta = 0.95
epsilon = 1e-07
TILE = 128
bf16 = jnp.bfloat16
f32 = jnp.float32


def merge_kernel(
    old_ref, new_ref, grad_ref, mom_ref, merged_ref, start_ref, old, new, grad, mom, merged, sems, done
):
    loads = [
        pltpu.make_async_copy(source, target, sems.at[at])
        for at, (source, target) in enumerate(
            [(mom_ref, mom), (grad_ref, grad), (old_ref, old), (new_ref, new)]
        )
    ]
    for load in loads:
        load.start()
    for load in loads:
        load.wait()
    for j in range(grad.shape[0]):
        slot = new[j]
        value = beta * mom[old[j]] + grad[slot].astype(f32)
        start_ref[slot] = value.astype(bf16)
        merged[slot] = value
    store = pltpu.make_async_copy(merged, merged_ref, done)
    store.start()
    store.wait()


def merge(grad, momentum, old_slot, new_slot):
    hbm = pl.BlockSpec(memory_space=pltpu.HBM)
    return pl.pallas_call(
        merge_kernel,
        out_shape=(
            jax.ShapeDtypeStruct(momentum.shape, f32),
            jax.ShapeDtypeStruct(grad.shape, bf16),
        ),
        in_specs=[hbm] * 4,
        out_specs=(hbm, pl.BlockSpec(memory_space=pltpu.VMEM)),
        scratch_shapes=[
            pltpu.SMEM(old_slot.shape, jnp.int32),
            pltpu.SMEM(new_slot.shape, jnp.int32),
            pltpu.VMEM(grad.shape, bf16),
            pltpu.VMEM(momentum.shape, f32),
            pltpu.VMEM(momentum.shape, f32),
            pltpu.SemaphoreType.DMA((4,)),
            pltpu.SemaphoreType.DMA,
        ],
        compiler_params=pltpu.CompilerParams(vmem_limit_bytes=63 << 20),
    )(old_slot, new_slot, grad, momentum)


def upper(count):
    return [(r, s) for r in range(count) for s in range(r, count)]


def gram_kernel(x_ref, out_ref):
    x = x_ref[...]
    gram = lax.dot_general(x, x, (((1,), (1,)), ((), ())), preferred_element_type=f32)
    for at, (r, s) in enumerate(upper(x.shape[0] // TILE)):
        block = gram[r * TILE : (r + 1) * TILE, s * TILE : (s + 1) * TILE]
        out_ref[at * TILE : (at + 1) * TILE, :] = block


def sum_kernel(parts_ref, out_ref):
    total = parts_ref[0]
    for k in range(1, parts_ref.shape[0]):
        total += parts_ref[k]
    for k in range(parts_ref.shape[0]):
        out_ref[k] = total


def split(value):
    high = value.astype(bf16)
    return high, (value - high.astype(f32)).astype(bf16)


def dot(left, right):
    return jnp.dot(left, right, preferred_element_type=f32)


def product(left, right):
    (lh, ll), (rh, rl) = left, right
    return dot(jnp.concatenate([lh, ll, lh], axis=1), jnp.concatenate([rh, rh, rl], axis=0))


def symmetric(left, right):
    half = left[0].shape[0] // 2
    top = product([p[:half] for p in left], right)
    corner = product([p[half:] for p in left], [p[:, half:] for p in right])
    return jnp.concatenate([top, jnp.concatenate([top[:, half:].T, corner], axis=1)], axis=0)


def polish_kernel(width, packed_ref, x_ref, out_ref, gram_ref):
    rows = x_ref.shape[0]
    for at, (r, s) in enumerate(upper(rows // TILE)):
        block = packed_ref[at * TILE : (at + 1) * TILE, :]
        gram_ref[r * TILE : (r + 1) * TILE, s * TILE : (s + 1) * TILE] = block
        if r != s:
            gram_ref[s * TILE : (s + 1) * TILE, r * TILE : (r + 1) * TILE] = block.T
    gram = gram_ref[...]
    row = lax.broadcasted_iota(jnp.int32, (rows, rows), 0)
    column = lax.broadcasted_iota(jnp.int32, (rows, rows), 1)
    diagonal = row == column
    total = jnp.sum(jnp.where(diagonal, gram, 0.0))
    inverse = 1.0 / (jnp.sqrt(jnp.full((1, 1), total)) + epsilon)
    gram = gram * inverse * inverse
    rests, steps = [], []
    for step in range(3):
        g = split(gram)
        rest = coef_b * gram + coef_c * symmetric(g, g)
        q = split(rest)
        rests.append(rest)
        steps.append(q)
        if step < 2:
            half = coef_a * gram + symmetric(g, q)
        if step == 1:
            both = coef_a * (rests[0] + rests[1]) + symmetric(q, steps[0])
            both += jnp.where(diagonal, coef_a * coef_a, 0.0)
        if step < 2:
            gram = coef_a * half + symmetric(split(half), q)
    whole = split(coef_a * both + symmetric(steps[2], split(both)))
    x = x_ref[...]
    current = dot(whole[0], x) + dot(whole[1], x)
    out_ref[...] = (0.2 * math.sqrt(width) * inverse * current).astype(bf16)


def keep_kernel(in_ref, out_ref, done):
    copy = pltpu.make_async_copy(in_ref, out_ref, done)
    copy.start()
    copy.wait()


def keep(value):
    return pl.pallas_call(
        keep_kernel,
        out_shape=jax.ShapeDtypeStruct(value.shape, value.dtype),
        in_specs=[pl.BlockSpec(memory_space=pl.ANY)],
        out_specs=pl.BlockSpec(memory_space=pltpu.HBM),
        scratch_shapes=[pltpu.SemaphoreType.DMA],
        compiler_params=pltpu.CompilerParams(vmem_limit_bytes=16 << 20),
    )(value)


def polish(start, parts):
    rows, columns = start.shape
    vmem = pl.BlockSpec(memory_space=pltpu.VMEM)
    params = pltpu.CompilerParams(vmem_limit_bytes=48 << 20)
    blocks = len(upper(rows // TILE))
    packed = pl.pallas_call(
        gram_kernel,
        out_shape=jax.ShapeDtypeStruct((blocks * TILE, TILE), f32),
        in_specs=[vmem],
        out_specs=vmem,
        compiler_params=params,
    )(start)
    shares = packed.reshape(parts, blocks * TILE // parts, TILE)
    shares = lax.all_to_all(shares, "mp", split_axis=0, concat_axis=0, tiled=True)
    copies = pl.pallas_call(
        sum_kernel,
        out_shape=jax.ShapeDtypeStruct(shares.shape, f32),
        in_specs=[vmem],
        out_specs=vmem,
        compiler_params=params,
    )(shares)
    copies = lax.all_to_all(copies, "mp", split_axis=0, concat_axis=0, tiled=True)
    return pl.pallas_call(
        lambda *refs: polish_kernel(columns * parts, *refs),
        out_shape=jax.ShapeDtypeStruct(start.shape, bf16),
        in_specs=[vmem, vmem],
        out_specs=vmem,
        scratch_shapes=[pltpu.VMEM((rows, rows), f32)],
        compiler_params=params,
    )(copies.reshape(blocks * TILE, TILE), start)


def body(grad, momentum, old_slot, new_slot):
    merged, start = merge(grad, momentum, old_slot, new_slot)
    got = lax.all_to_all(start, "dp", split_axis=0, concat_axis=0, tiled=True)
    slots, rows, columns = got.shape
    update = polish(got.reshape(slots * rows, columns), lax.axis_size("mp"))
    update = update.reshape(slots, rows, columns)
    return merged, keep(lax.all_to_all(update, "dp", split_axis=0, concat_axis=0, tiled=True))


def solution(mesh):
    placed = (P(None, "dp", "mp"), P(None, "dp", "mp"), P(), P())
    return jax.shard_map(
        body,
        mesh=mesh,
        in_specs=placed,
        out_specs=(P(None, "dp", "mp"), P(None, "dp", "mp")),
        check_vma=False,
    )
```

```python
import math

import jax
import jax.numpy as jnp
from jax import lax
from jax.experimental import pallas as pl
from jax.experimental.pallas import tpu as pltpu
from jax.sharding import PartitionSpec as P

coef_a = 3.4445
coef_b = -4.775
coef_c = 2.0315
beta = 0.95
epsilon = 1e-07
TILE = 128
bf16 = jnp.bfloat16
f32 = jnp.float32


def merge_kernel(
    old_ref, new_ref, grad_ref, mom_ref, merged_ref, start_ref, old, new, grad, mom, sems
):
    loads = [
        pltpu.make_async_copy(source, target, sems.at[at])
        for at, (source, target) in enumerate(
            [(mom_ref, mom), (grad_ref, grad), (old_ref, old), (new_ref, new)]
        )
    ]
    for load in loads:
        load.start()
    for load in loads:
        load.wait()
    for j in range(grad.shape[0]):
        slot = new[j]
        value = beta * mom[old[j]] + grad[slot].astype(f32)
        start_ref[slot] = value.astype(bf16)
        merged_ref[slot] = value


def merge(grad, momentum, old_slot, new_slot):
    hbm = pl.BlockSpec(memory_space=pltpu.HBM)
    return pl.pallas_call(
        merge_kernel,
        out_shape=(
            jax.ShapeDtypeStruct(momentum.shape, f32),
            jax.ShapeDtypeStruct(grad.shape, bf16),
        ),
        in_specs=[hbm] * 4,
        out_specs=(pl.BlockSpec(memory_space=pltpu.VMEM),) * 2,
        scratch_shapes=[
            pltpu.SMEM(old_slot.shape, jnp.int32),
            pltpu.SMEM(new_slot.shape, jnp.int32),
            pltpu.VMEM(grad.shape, bf16),
            pltpu.VMEM(momentum.shape, f32),
            pltpu.SemaphoreType.DMA((4,)),
        ],
        compiler_params=pltpu.CompilerParams(vmem_limit_bytes=32 << 20),
    )(*(pltpu.with_memory_space_constraint(x, pltpu.HBM) for x in (old_slot, new_slot, grad, momentum)))


def upper(count):
    return [(r, s) for r in range(count) for s in range(r, count)]


def exponent(bound):
    return jnp.floor(jnp.log(jnp.maximum(bound, 1e-30)) * (1.0 / math.log(2.0))) - 14.0


def power(value):
    return jnp.exp(value * math.log(2.0))


def spot(rows):
    row = lax.broadcasted_iota(jnp.int32, (rows, TILE), 0)
    return (row % 8 == 7) & (lax.broadcasted_iota(jnp.int32, (rows, TILE), 1) == 0)


def gram_kernel(x_ref, out_ref):
    x = x_ref[...]
    gram = lax.dot_general(x, x, (((1,), (1,)), ((), ())), preferred_element_type=f32)
    wide = x.astype(f32)
    bound = jnp.max(jnp.sum(wide * wide, axis=1, keepdims=True), axis=0, keepdims=True)
    power_of = exponent(bound)
    gram = gram * power(-power_of)
    parts = out_ref.shape[0]
    for at, (r, s) in enumerate(upper(x.shape[0] // TILE)):
        block = gram[r * TILE : (r + 1) * TILE, s * TILE : (s + 1) * TILE]
        if at == 0:
            block = jnp.where(spot(TILE), power_of, block)
        out_ref[:, at * 8 : (at + 1) * 8, :] = block.reshape(parts, 8, TILE)


def sum_kernel(parts_ref, out_ref):
    total = jnp.zeros(out_ref.shape, f32)
    for k in range(parts_ref.shape[0]):
        total += parts_ref[k] * power(parts_ref[k, 7:8, 0:1])
    row = lax.broadcasted_iota(jnp.int32, out_ref.shape, 0)
    marks = (row == 7) & (lax.broadcasted_iota(jnp.int32, out_ref.shape, 1) == 0)
    total = jnp.where(marks, 0.0, total)
    bound = jnp.max(jnp.max(jnp.abs(total), axis=1, keepdims=True), axis=0, keepdims=True)
    power_of = exponent(bound)
    out_ref[...] = jnp.where(marks, power_of, total * power(-power_of))


def split(value):
    high = value.astype(bf16)
    return high, (value - high.astype(f32)).astype(bf16)


def dot(left, right):
    return jnp.dot(left, right, preferred_element_type=f32)


def product(left, right):
    (lh, ll), (rh, rl) = left, right
    return dot(jnp.concatenate([lh, ll, lh], axis=1), jnp.concatenate([rh, rh, rl], axis=0))


def symmetric(left, right):
    half = left[0].shape[0] // 2
    top = product([p[:half] for p in left], right)
    corner = product([p[half:] for p in left], [p[:, half:] for p in right])
    return jnp.concatenate([top, jnp.concatenate([top[:, half:].T, corner], axis=1)], axis=0)


def polish_kernel(width, packed_ref, x_ref, merged_ref, out_ref, kept_ref, gram_ref, done):
    store = pltpu.make_async_copy(merged_ref, kept_ref, done)
    store.start()
    rows = x_ref.shape[0]
    parts = packed_ref.shape[0]
    scale = power(packed_ref[:, 7:8, 0:1])
    row = lax.broadcasted_iota(jnp.int32, (TILE, TILE), 0)
    below = row > lax.broadcasted_iota(jnp.int32, (TILE, TILE), 1)
    for at, (r, s) in enumerate(upper(rows // TILE)):
        block = (packed_ref[:, at * 8 : (at + 1) * 8, :] * scale).reshape(TILE, TILE)
        if r == s:
            block = jnp.where(below, block.T, block)
        gram_ref[r * TILE : (r + 1) * TILE, s * TILE : (s + 1) * TILE] = block
        if r != s:
            gram_ref[s * TILE : (s + 1) * TILE, r * TILE : (r + 1) * TILE] = block.T
    gram = gram_ref[...]
    row = lax.broadcasted_iota(jnp.int32, (rows, rows), 0)
    column = lax.broadcasted_iota(jnp.int32, (rows, rows), 1)
    diagonal = row == column
    total = jnp.sum(jnp.where(diagonal, gram, 0.0))
    inverse = 1.0 / (jnp.sqrt(jnp.full((1, 1), total)) + epsilon)
    gram = gram * inverse * inverse
    rests, steps = [], []
    for step in range(3):
        g = split(gram)
        rest = coef_b * gram + coef_c * symmetric(g, g)
        q = split(rest)
        rests.append(rest)
        steps.append(q)
        if step < 2:
            half = coef_a * gram + symmetric(g, q)
        if step == 1:
            both = coef_a * (rests[0] + rests[1]) + symmetric(q, steps[0])
            both += jnp.where(diagonal, coef_a * coef_a, 0.0)
        if step < 2:
            gram = coef_a * half + symmetric(split(half), q)
    whole = split(coef_a * both + symmetric(steps[2], split(both)))
    x = x_ref[...]
    current = dot(whole[0], x) + dot(whole[1], x)
    out_ref[...] = (0.2 * math.sqrt(width) * inverse * current).astype(bf16)
    store.wait()


def keep_kernel(in_ref, out_ref, done):
    copy = pltpu.make_async_copy(in_ref, out_ref, done)
    copy.start()
    copy.wait()


def keep(value):
    return pl.pallas_call(
        keep_kernel,
        out_shape=jax.ShapeDtypeStruct(value.shape, value.dtype),
        in_specs=[pl.BlockSpec(memory_space=pl.ANY)],
        out_specs=pl.BlockSpec(memory_space=pltpu.HBM),
        scratch_shapes=[pltpu.SemaphoreType.DMA],
        compiler_params=pltpu.CompilerParams(vmem_limit_bytes=16 << 20),
    )(value)


def polish(start, merged, parts):
    rows, columns = start.shape
    vmem = pl.BlockSpec(memory_space=pltpu.VMEM)
    params = pltpu.CompilerParams(vmem_limit_bytes=48 << 20)
    share = (len(upper(rows // TILE)) * 8, TILE)
    packed = pl.pallas_call(
        gram_kernel,
        out_shape=jax.ShapeDtypeStruct((parts, *share), f32),
        in_specs=[vmem],
        out_specs=vmem,
        compiler_params=params,
    )(start)
    packed = packed.astype(jnp.float16)
    packed = lax.all_to_all(packed, "mp", split_axis=0, concat_axis=0, tiled=True)
    total = pl.pallas_call(
        sum_kernel,
        out_shape=jax.ShapeDtypeStruct(share, f32),
        in_specs=[vmem],
        out_specs=vmem,
        compiler_params=params,
    )(packed.astype(f32))
    copies = jnp.broadcast_to(total.astype(jnp.float16), (parts, *share))
    copies = lax.all_to_all(copies, "mp", split_axis=0, concat_axis=0, tiled=True)
    return pl.pallas_call(
        lambda *refs: polish_kernel(columns * parts, *refs),
        out_shape=(
            jax.ShapeDtypeStruct(start.shape, bf16),
            jax.ShapeDtypeStruct(merged.shape, f32),
        ),
        in_specs=[vmem] * 3,
        out_specs=(vmem, pl.BlockSpec(memory_space=pltpu.HBM)),
        scratch_shapes=[pltpu.VMEM((rows, rows), f32), pltpu.SemaphoreType.DMA],
        compiler_params=params,
    )(copies.astype(f32), start, merged)


def body(grad, momentum, old_slot, new_slot):
    merged, start = merge(grad, momentum, old_slot, new_slot)
    got = lax.all_to_all(start, "dp", split_axis=0, concat_axis=0, tiled=True)
    slots, rows, columns = got.shape
    update, merged = polish(got.reshape(slots * rows, columns), merged, lax.axis_size("mp"))
    update = update.reshape(slots, rows, columns)
    return merged, keep(lax.all_to_all(update, "dp", split_axis=0, concat_axis=0, tiled=True))


def solution(mesh):
    placed = (P(None, "dp", "mp"), P(None, "dp", "mp"), P(), P())
    return jax.shard_map(
        body,
        mesh=mesh,
        in_specs=placed,
        out_specs=(P(None, "dp", "mp"), P(None, "dp", "mp")),
        check_vma=False,
    )
```

```python
import math

import jax
import jax.numpy as jnp
from jax import lax
from jax.experimental import pallas as pl
from jax.experimental.pallas import tpu as pltpu
from jax.sharding import PartitionSpec as P

coef_a = 3.4445
coef_b = -4.775
coef_c = 2.0315
beta = 0.95
epsilon = 1e-07
TILE = 128
bf16 = jnp.bfloat16
f32 = jnp.float32


def merge_kernel(
    old_ref, new_ref, grad_ref, mom_ref, merged_ref, start_ref, old, new, grad, mom, sems
):
    loads = [
        pltpu.make_async_copy(source, target, sems.at[at])
        for at, (source, target) in enumerate(
            [(mom_ref, mom), (grad_ref, grad), (old_ref, old), (new_ref, new)]
        )
    ]
    for load in loads:
        load.start()
    for load in loads:
        load.wait()
    for j in range(grad.shape[0]):
        slot = new[j]
        value = beta * mom[old[j]] + grad[slot].astype(f32)
        start_ref[slot] = value.astype(bf16)
        merged_ref[slot] = value


def merge(grad, momentum, old_slot, new_slot):
    hbm = pl.BlockSpec(memory_space=pltpu.HBM)
    return pl.pallas_call(
        merge_kernel,
        out_shape=(
            jax.ShapeDtypeStruct(momentum.shape, f32),
            jax.ShapeDtypeStruct(grad.shape, bf16),
        ),
        in_specs=[hbm] * 4,
        out_specs=(pl.BlockSpec(memory_space=pltpu.VMEM),) * 2,
        scratch_shapes=[
            pltpu.SMEM(old_slot.shape, jnp.int32),
            pltpu.SMEM(new_slot.shape, jnp.int32),
            pltpu.VMEM(grad.shape, bf16),
            pltpu.VMEM(momentum.shape, f32),
            pltpu.SemaphoreType.DMA((4,)),
        ],
        compiler_params=pltpu.CompilerParams(vmem_limit_bytes=32 << 20),
    )(*(pltpu.with_memory_space_constraint(x, pltpu.HBM) for x in (old_slot, new_slot, grad, momentum)))


def upper(count):
    return [(r, s) for r in range(count) for s in range(r, count)]


def exponent(bound):
    return jnp.floor(jnp.log(jnp.maximum(bound, 1e-30)) * (1.0 / math.log(2.0))) - 14.0


def power(value):
    return jnp.exp(value * math.log(2.0))


def spot(rows):
    row = lax.broadcasted_iota(jnp.int32, (rows, TILE), 0)
    return (row % 8 == 7) & (lax.broadcasted_iota(jnp.int32, (rows, TILE), 1) == 0)


def gram_kernel(x_ref, out_ref):
    x = x_ref[...]
    gram = lax.dot_general(x, x, (((1,), (1,)), ((), ())), preferred_element_type=f32)
    wide = x.astype(f32)
    bound = jnp.max(jnp.sum(wide * wide, axis=1, keepdims=True), axis=0, keepdims=True)
    power_of = exponent(bound)
    gram = gram * power(-power_of)
    parts = out_ref.shape[0]
    for at, (r, s) in enumerate(upper(x.shape[0] // TILE)):
        block = gram[r * TILE : (r + 1) * TILE, s * TILE : (s + 1) * TILE]
        if at == 0:
            block = jnp.where(spot(TILE), power_of, block)
        out_ref[:, at * 8 : (at + 1) * 8, :] = block.reshape(parts, 8, TILE)


def sum_kernel(parts_ref, out_ref):
    total = jnp.zeros(out_ref.shape, f32)
    for k in range(parts_ref.shape[0]):
        total += parts_ref[k] * power(parts_ref[k, 7:8, 0:1])
    row = lax.broadcasted_iota(jnp.int32, out_ref.shape, 0)
    marks = (row == 7) & (lax.broadcasted_iota(jnp.int32, out_ref.shape, 1) == 0)
    total = jnp.where(marks, 0.0, total)
    bound = jnp.max(jnp.max(jnp.abs(total), axis=1, keepdims=True), axis=0, keepdims=True)
    power_of = exponent(bound)
    out_ref[...] = jnp.where(marks, power_of, total * power(-power_of))


def split(value):
    high = value.astype(bf16)
    return high, (value - high.astype(f32)).astype(bf16)


def dot(left, right):
    return jnp.dot(left, right, preferred_element_type=f32)


def product(left, right):
    (lh, ll), (rh, rl) = left, right
    return dot(jnp.concatenate([lh, ll, lh], axis=1), jnp.concatenate([rh, rh, rl], axis=0))


def symmetric(left, right):
    half = left[0].shape[0] // 2
    top = product([p[:half] for p in left], right)
    corner = product([p[half:] for p in left], [p[:, half:] for p in right])
    return jnp.concatenate([top, jnp.concatenate([top[:, half:].T, corner], axis=1)], axis=0)


def polish_kernel(width, packed_ref, x_ref, merged_ref, out_ref, kept_ref, gram_ref, done):
    store = pltpu.make_async_copy(merged_ref, kept_ref, done)
    store.start()
    rows = x_ref.shape[0]
    parts = packed_ref.shape[0]
    scale = power(packed_ref[:, 7:8, 0:1])
    row = lax.broadcasted_iota(jnp.int32, (TILE, TILE), 0)
    below = row > lax.broadcasted_iota(jnp.int32, (TILE, TILE), 1)
    for at, (r, s) in enumerate(upper(rows // TILE)):
        block = (packed_ref[:, at * 8 : (at + 1) * 8, :] * scale).reshape(TILE, TILE)
        if r == s:
            block = jnp.where(below, block.T, block)
        gram_ref[r * TILE : (r + 1) * TILE, s * TILE : (s + 1) * TILE] = block
        if r != s:
            gram_ref[s * TILE : (s + 1) * TILE, r * TILE : (r + 1) * TILE] = block.T
    gram = gram_ref[...]
    row = lax.broadcasted_iota(jnp.int32, (rows, rows), 0)
    column = lax.broadcasted_iota(jnp.int32, (rows, rows), 1)
    diagonal = row == column
    total = jnp.sum(jnp.where(diagonal, gram, 0.0))
    inverse = 1.0 / (jnp.sqrt(jnp.full((1, 1), total)) + epsilon)
    gram = gram * inverse * inverse
    rests, steps = [], []
    for step in range(3):
        g = split(gram)
        rest = coef_b * gram + coef_c * symmetric(g, g)
        q = split(rest)
        rests.append(rest)
        steps.append(q)
        if step < 2:
            half = coef_a * gram + symmetric(g, q)
        if step == 1:
            both = coef_a * (rests[0] + rests[1]) + symmetric(q, steps[0])
            both += jnp.where(diagonal, coef_a * coef_a, 0.0)
        if step < 2:
            gram = coef_a * half + symmetric(split(half), q)
    whole = split(coef_a * both + symmetric(steps[2], split(both)))
    x = x_ref[...]
    current = dot(whole[0], x) + dot(whole[1], x)
    out_ref[...] = (0.2 * math.sqrt(width) * inverse * current).astype(bf16)
    store.wait()


def keep_kernel(in_ref, out_ref, done):
    copy = pltpu.make_async_copy(in_ref, out_ref, done)
    copy.start()
    copy.wait()


def keep(value):
    return pl.pallas_call(
        keep_kernel,
        out_shape=jax.ShapeDtypeStruct(value.shape, value.dtype),
        in_specs=[pl.BlockSpec(memory_space=pl.ANY)],
        out_specs=pl.BlockSpec(memory_space=pltpu.HBM),
        scratch_shapes=[pltpu.SemaphoreType.DMA],
        compiler_params=pltpu.CompilerParams(vmem_limit_bytes=16 << 20),
    )(value)


def polish(start, merged, parts):
    rows, columns = start.shape
    vmem = pl.BlockSpec(memory_space=pltpu.VMEM)
    params = pltpu.CompilerParams(vmem_limit_bytes=48 << 20)
    share = (len(upper(rows // TILE)) * 8, TILE)
    packed = pl.pallas_call(
        gram_kernel,
        out_shape=jax.ShapeDtypeStruct((parts, *share), f32),
        in_specs=[vmem],
        out_specs=vmem,
        compiler_params=params,
    )(start)
    packed = packed.astype(jnp.float16)
    packed = lax.all_to_all(packed, "mp", split_axis=0, concat_axis=0, tiled=True)
    total = pl.pallas_call(
        sum_kernel,
        out_shape=jax.ShapeDtypeStruct(share, f32),
        in_specs=[vmem],
        out_specs=vmem,
        compiler_params=params,
    )(packed.astype(f32))
    copies = jnp.broadcast_to(total.astype(jnp.float16), (parts, *share))
    copies = lax.all_to_all(copies, "mp", split_axis=0, concat_axis=0, tiled=True)
    return pl.pallas_call(
        lambda *refs: polish_kernel(columns * parts, *refs),
        out_shape=(
            jax.ShapeDtypeStruct(start.shape, bf16),
            jax.ShapeDtypeStruct(merged.shape, f32),
        ),
        in_specs=[vmem] * 3,
        out_specs=(vmem, pl.BlockSpec(memory_space=pltpu.HBM)),
        scratch_shapes=[pltpu.VMEM((rows, rows), f32), pltpu.SemaphoreType.DMA],
        compiler_params=params,
    )(copies.astype(f32), start, merged)


def exchange(value):
    order = [device ^ 1 for device in range(value.shape[0])]
    return lax.all_to_all(value, "dp", split_axis=0, concat_axis=0, tiled=True, axis_index_groups=[order])


def body(grad, momentum, old_slot, new_slot):
    merged, start = merge(grad, momentum, old_slot, new_slot)
    got = exchange(start)
    slots, rows, columns = got.shape
    update, merged = polish(got.reshape(slots * rows, columns), merged, lax.axis_size("mp"))
    update = update.reshape(slots, rows, columns)
    return merged, keep(exchange(update))


def solution(mesh):
    placed = (P(None, "dp", "mp"), P(None, "dp", "mp"), P(), P())
    return jax.shard_map(
        body,
        mesh=mesh,
        in_specs=placed,
        out_specs=(P(None, "dp", "mp"), P(None, "dp", "mp")),
        check_vma=False,
    )
```

```python
import math

import jax
import jax.numpy as jnp
from jax import lax
from jax.experimental import pallas as pl
from jax.experimental.pallas import tpu as pltpu
from jax.sharding import PartitionSpec as P

coef_a = 3.4445
coef_b = -4.775
coef_c = 2.0315
beta = 0.95
epsilon = 1e-07
TILE = 128
CHUNK = 32
bf16 = jnp.bfloat16
f32 = jnp.float32
f8 = jnp.float8_e4m3fn


def merge_kernel(
    old_ref, new_ref, grad_ref, mom_ref, merged_ref, start_ref, old, new, grad, mom, sems
):
    loads = [
        pltpu.make_async_copy(source, target, sems.at[at])
        for at, (source, target) in enumerate(
            [(mom_ref, mom), (grad_ref, grad), (old_ref, old), (new_ref, new)]
        )
    ]
    for load in loads:
        load.start()
    for load in loads:
        load.wait()
    for j in range(grad.shape[0]):
        slot = new[j]
        value = beta * mom[old[j]] + grad[slot].astype(f32)
        start_ref[slot] = value.astype(bf16)
        merged_ref[slot] = value


def merge(grad, momentum, old_slot, new_slot):
    hbm = pl.BlockSpec(memory_space=pltpu.HBM)
    return pl.pallas_call(
        merge_kernel,
        out_shape=(
            jax.ShapeDtypeStruct(momentum.shape, f32),
            jax.ShapeDtypeStruct(grad.shape, bf16),
        ),
        in_specs=[hbm] * 4,
        out_specs=(pl.BlockSpec(memory_space=pltpu.VMEM),) * 2,
        scratch_shapes=[
            pltpu.SMEM(old_slot.shape, jnp.int32),
            pltpu.SMEM(new_slot.shape, jnp.int32),
            pltpu.VMEM(grad.shape, bf16),
            pltpu.VMEM(momentum.shape, f32),
            pltpu.SemaphoreType.DMA((4,)),
        ],
        compiler_params=pltpu.CompilerParams(vmem_limit_bytes=32 << 20),
    )(*(pltpu.with_memory_space_constraint(x, pltpu.HBM) for x in (old_slot, new_slot, grad, momentum)))


def upper(count):
    return [(r, s) for r in range(count) for s in range(r, count)]


def exponent(bound):
    return jnp.floor(jnp.log(jnp.maximum(bound, 1e-30)) * (1.0 / math.log(2.0))) - 14.0


def power(value):
    return jnp.exp(value * math.log(2.0))


def spot(rows):
    row = lax.broadcasted_iota(jnp.int32, (rows, TILE), 0)
    return (row % 8 == 7) & (lax.broadcasted_iota(jnp.int32, (rows, TILE), 1) == 0)


def gram_kernel(x_ref, out_ref):
    x = x_ref[...]
    gram = lax.dot_general(x, x, (((1,), (1,)), ((), ())), preferred_element_type=f32)
    wide = x.astype(f32)
    bound = jnp.max(jnp.sum(wide * wide, axis=1, keepdims=True), axis=0, keepdims=True)
    power_of = exponent(bound)
    gram = gram * power(-power_of)
    parts = out_ref.shape[0]
    for at, (r, s) in enumerate(upper(x.shape[0] // TILE)):
        block = gram[r * TILE : (r + 1) * TILE, s * TILE : (s + 1) * TILE]
        if at == 0:
            block = jnp.where(spot(TILE), power_of, block)
        out_ref[:, at * 8 : (at + 1) * 8, :] = block.reshape(parts, 8, TILE)


def sum_kernel(parts_ref, out_ref):
    total = jnp.zeros(out_ref.shape, f32)
    for k in range(parts_ref.shape[0]):
        total += parts_ref[k] * power(parts_ref[k, 7:8, 0:1])
    row = lax.broadcasted_iota(jnp.int32, out_ref.shape, 0)
    marks = (row == 7) & (lax.broadcasted_iota(jnp.int32, out_ref.shape, 1) == 0)
    total = jnp.where(marks, 0.0, total)
    bound = jnp.max(jnp.max(jnp.abs(total), axis=1, keepdims=True), axis=0, keepdims=True)
    power_of = exponent(bound)
    out_ref[...] = jnp.where(marks, power_of, total * power(-power_of))


def put(form, value, row, column, power_of):
    high_ref, left_ref, right_ref = form
    size = high_ref.shape[0]
    columns = slice(column, column + value.shape[1])
    later = slice(size + column, size + column + value.shape[1])
    for at in range(0, value.shape[0], CHUNK):
        chunk = value[at : at + CHUNK]
        high = chunk.astype(bf16)
        coarse = (chunk * 2.0**power_of).astype(f8)
        low = ((chunk - high.astype(f32)) * 2.0 ** (power_of + 8)).astype(f8)
        lines = slice(row + at, row + at + CHUNK)
        high_ref[lines, columns] = high
        left_ref[lines, columns] = coarse
        left_ref[lines, later] = low
        right_ref[lines, columns] = low
        right_ref[slice(size + row + at, size + row + at + CHUNK), columns] = coarse


def dot(left, right):
    return jnp.dot(left, right, preferred_element_type=f32)


def product(left, right, rows, columns, power_of):
    main = dot(left[0][rows, :], right[0][:, columns])
    return main + dot(left[1][rows, :], right[2][:, columns]) * 2.0 ** -(power_of + 8)


def polish_kernel(width, packed_ref, x_ref, merged_ref, out_ref, kept_ref, *scratch):
    gram_ref, half_ref, rest_ref, pair_ref, done = scratch[:5]
    gram_form, first_form, half_form, second_form, pair_form = (scratch[at : at + 3] for at in range(5, 20, 3))
    store = pltpu.make_async_copy(merged_ref, kept_ref, done)
    store.start()
    size = x_ref.shape[0]
    front, back = slice(0, size // 2), slice(size // 2, size)
    blocks = ((front, front), (front, back), (back, back))

    scale = power(packed_ref[:, 7:8, 0:1])
    row = lax.broadcasted_iota(jnp.int32, (TILE, TILE), 0)
    column = lax.broadcasted_iota(jnp.int32, (TILE, TILE), 1)
    total = jnp.zeros((1, 1), f32)
    for at, (r, s) in enumerate(upper(size // TILE)):
        block = (packed_ref[:, at * 8 : (at + 1) * 8, :] * scale).reshape(TILE, TILE)
        if r == s:
            block = jnp.where(row > column, block.T, block)
            total += jnp.sum(jnp.where(row == column, block, 0.0), keepdims=True)
        gram_ref[r * TILE : (r + 1) * TILE, s * TILE : (s + 1) * TILE] = block
        if r != s:
            gram_ref[s * TILE : (s + 1) * TILE, r * TILE : (r + 1) * TILE] = block.T
    inverse = 1.0 / (jnp.sqrt(total) + epsilon)
    for at in range(0, size, CHUNK):
        chunk = gram_ref[at : at + CHUNK, :] * inverse * inverse
        gram_ref[at : at + CHUNK, :] = chunk
        put(gram_form, chunk, at, 0, 7)

    def symmetric(left, right, power_of, finish, form, form_power, kept=None):
        for rows, columns in blocks:
            value = finish(product(left, right, rows, columns, power_of), rows, columns)
            if kept is not None:
                kept[rows, columns] = value
            put(form, value, rows.start, columns.start, form_power)
            if rows != columns:
                put(form, value.T, columns.start, rows.start, form_power)

    def rest(step):
        def finish(square, rows, columns):
            value = coef_b * gram_ref[rows, columns] + coef_c * square
            if step == 0:
                rest_ref[rows, columns] = coef_a * value
            if step == 1:
                rest_ref[rows, columns] = rest_ref[rows, columns] + coef_a * value
            return value

        return finish

    def pair(value, rows, columns):
        value = rest_ref[rows, columns] + value
        if rows == columns:
            line = lax.broadcasted_iota(jnp.int32, value.shape, 0)
            value += jnp.where(line == lax.broadcasted_iota(jnp.int32, value.shape, 1), coef_a**2, 0.0)
        return value

    once = lambda value, rows, columns: coef_a * gram_ref[rows, columns] + value
    twice = lambda value, rows, columns: coef_a * half_ref[rows, columns] + value
    symmetric(gram_form, gram_form, 14, rest(0), first_form, 7)
    symmetric(gram_form, first_form, 14, once, half_form, 7, half_ref)
    symmetric(half_form, first_form, 14, twice, gram_form, 7, gram_ref)
    symmetric(gram_form, gram_form, 14, rest(1), second_form, 7)
    symmetric(gram_form, second_form, 14, once, half_form, 7, half_ref)
    symmetric(second_form, first_form, 14, pair, pair_form, 5, pair_ref)
    symmetric(half_form, second_form, 14, twice, gram_form, 7, gram_ref)
    symmetric(gram_form, gram_form, 14, rest(2), first_form, 7)
    near, across, far = (coef_a * pair_ref[r, c] + product(first_form, pair_form, r, c, 12) for r, c in blocks)
    x = x_ref[...]
    for rows, lines in ((front, (near, across)), (back, (across.T, far))):
        whole = jnp.concatenate(lines, axis=1)
        high = whole.astype(bf16)
        current = dot(high, x) + dot((whole - high.astype(f32)).astype(bf16), x)
        out_ref[rows] = (0.2 * math.sqrt(width) * inverse * current).astype(bf16)
    store.wait()


def keep_kernel(in_ref, out_ref, done):
    copy = pltpu.make_async_copy(in_ref, out_ref, done)
    copy.start()
    copy.wait()


def keep(value):
    return pl.pallas_call(
        keep_kernel,
        out_shape=jax.ShapeDtypeStruct(value.shape, value.dtype),
        in_specs=[pl.BlockSpec(memory_space=pl.ANY)],
        out_specs=pl.BlockSpec(memory_space=pltpu.HBM),
        scratch_shapes=[pltpu.SemaphoreType.DMA],
        compiler_params=pltpu.CompilerParams(vmem_limit_bytes=16 << 20),
    )(value)


def polish(start, merged, parts):
    rows, columns = start.shape
    vmem = pl.BlockSpec(memory_space=pltpu.VMEM)
    params = pltpu.CompilerParams(vmem_limit_bytes=48 << 20)
    share = (len(upper(rows // TILE)) * 8, TILE)
    packed = pl.pallas_call(
        gram_kernel,
        out_shape=jax.ShapeDtypeStruct((parts, *share), f32),
        in_specs=[vmem],
        out_specs=vmem,
        compiler_params=params,
    )(start)
    packed = packed.astype(jnp.float16)
    packed = lax.all_to_all(packed, "mp", split_axis=0, concat_axis=0, tiled=True)
    total = pl.pallas_call(
        sum_kernel,
        out_shape=jax.ShapeDtypeStruct(share, f32),
        in_specs=[vmem],
        out_specs=vmem,
        compiler_params=params,
    )(packed.astype(f32))
    copies = jnp.broadcast_to(total.astype(jnp.float16), (parts, *share))
    copies = lax.all_to_all(copies, "mp", split_axis=0, concat_axis=0, tiled=True)
    return pl.pallas_call(
        lambda *refs: polish_kernel(columns * parts, *refs),
        out_shape=(
            jax.ShapeDtypeStruct(start.shape, bf16),
            jax.ShapeDtypeStruct(merged.shape, f32),
        ),
        in_specs=[vmem] * 3,
        out_specs=(vmem, pl.BlockSpec(memory_space=pltpu.HBM)),
        scratch_shapes=[pltpu.VMEM((rows, rows), f32)] * 4
        + [pltpu.SemaphoreType.DMA]
        + [pltpu.VMEM((rows, rows), bf16), pltpu.VMEM((rows, 2 * rows), f8), pltpu.VMEM((2 * rows, rows), f8)] * 5,
        compiler_params=params,
    )(copies.astype(f32), start, merged)


def exchange(value):
    order = [device ^ 1 for device in range(value.shape[0])]
    return lax.all_to_all(value, "dp", split_axis=0, concat_axis=0, tiled=True, axis_index_groups=[order])


def body(grad, momentum, old_slot, new_slot):
    merged, start = merge(grad, momentum, old_slot, new_slot)
    got = exchange(start)
    slots, rows, columns = got.shape
    update, merged = polish(got.reshape(slots * rows, columns), merged, lax.axis_size("mp"))
    update = update.reshape(slots, rows, columns)
    return merged, keep(exchange(update))


def solution(mesh):
    placed = (P(None, "dp", "mp"), P(None, "dp", "mp"), P(), P())
    return jax.shard_map(
        body,
        mesh=mesh,
        in_specs=placed,
        out_specs=(P(None, "dp", "mp"), P(None, "dp", "mp")),
        check_vma=False,
    )
```

```python
import math

import jax
import jax.numpy as jnp
from jax import lax
from jax.experimental import pallas as pl
from jax.experimental.pallas import tpu as pltpu
from jax.sharding import PartitionSpec as P

coef_a = 3.4445
coef_b = -4.775
coef_c = 2.0315
beta = 0.95
epsilon = 1e-07
TILE = 128
CHUNK = 32
bf16 = jnp.bfloat16
f32 = jnp.float32
f8 = jnp.float8_e4m3fn


def merge_kernel(
    old_ref, new_ref, grad_ref, mom_ref, merged_ref, start_ref, old, new, grad, mom, sems
):
    loads = [
        pltpu.make_async_copy(source, target, sems.at[at])
        for at, (source, target) in enumerate(
            [(mom_ref, mom), (grad_ref, grad), (old_ref, old), (new_ref, new)]
        )
    ]
    for load in loads:
        load.start()
    for load in loads:
        load.wait()
    for j in range(grad.shape[0]):
        slot = new[j]
        value = beta * mom[old[j]] + grad[slot].astype(f32)
        start_ref[slot] = value.astype(bf16)
        merged_ref[slot] = value


def merge(grad, momentum, old_slot, new_slot):
    hbm = pl.BlockSpec(memory_space=pltpu.HBM)
    return pl.pallas_call(
        merge_kernel,
        out_shape=(
            jax.ShapeDtypeStruct(momentum.shape, f32),
            jax.ShapeDtypeStruct(grad.shape, bf16),
        ),
        in_specs=[hbm] * 4,
        out_specs=(pl.BlockSpec(memory_space=pltpu.VMEM),) * 2,
        scratch_shapes=[
            pltpu.SMEM(old_slot.shape, jnp.int32),
            pltpu.SMEM(new_slot.shape, jnp.int32),
            pltpu.VMEM(grad.shape, bf16),
            pltpu.VMEM(momentum.shape, f32),
            pltpu.SemaphoreType.DMA((4,)),
        ],
        compiler_params=pltpu.CompilerParams(vmem_limit_bytes=32 << 20),
    )(*(pltpu.with_memory_space_constraint(x, pltpu.HBM) for x in (old_slot, new_slot, grad, momentum)))


def upper(count):
    return [(r, s) for r in range(count) for s in range(r, count)]


def exponent(bound):
    return jnp.floor(jnp.log(jnp.maximum(bound, 1e-30)) * (1.0 / math.log(2.0))) - 14.0


def power(value):
    return jnp.exp(value * math.log(2.0))


def spot(rows):
    row = lax.broadcasted_iota(jnp.int32, (rows, TILE), 0)
    return (row % 8 == 7) & (lax.broadcasted_iota(jnp.int32, (rows, TILE), 1) == 0)


def gram_kernel(x_ref, out_ref):
    x = x_ref[...]
    half = x.shape[0] // 2
    split = half // TILE
    dots = lambda p, q: lax.dot_general(p, q, (((1,), (1,)), ((), ())), preferred_element_type=f32)
    top, corner = dots(x[:half], x), dots(x[half:], x[half:])
    wide = x.astype(f32)
    bound = jnp.max(jnp.sum(wide * wide, axis=1, keepdims=True), axis=0, keepdims=True)
    power_of = exponent(bound)
    scale = power(-power_of)
    parts = out_ref.shape[0]
    for at, (r, s) in enumerate(upper(x.shape[0] // TILE)):
        gram, r, s = (top, r, s) if r < split else (corner, r - split, s - split)
        block = gram[r * TILE : (r + 1) * TILE, s * TILE : (s + 1) * TILE] * scale
        if at == 0:
            block = jnp.where(spot(TILE), power_of, block)
        out_ref[:, at * 8 : (at + 1) * 8, :] = block.reshape(parts, 8, TILE)


def sum_kernel(parts_ref, out_ref):
    powers = parts_ref[:, 7:8, 0:1]
    power_of = jnp.max(powers, axis=0) + math.ceil(math.log2(parts_ref.shape[0]))
    scales = power(powers - power_of)
    total = jnp.zeros(out_ref.shape, f32)
    for k in range(parts_ref.shape[0]):
        total += parts_ref[k] * scales[k]
    row = lax.broadcasted_iota(jnp.int32, out_ref.shape, 0)
    marks = (row == 7) & (lax.broadcasted_iota(jnp.int32, out_ref.shape, 1) == 0)
    out_ref[...] = jnp.where(marks, power_of, total)


def put(form, value, row, column, power_of):
    high_ref, left_ref, right_ref = form
    size = high_ref.shape[0]
    columns = slice(column, column + value.shape[1])
    later = slice(size + column, size + column + value.shape[1])
    for at in range(0, value.shape[0], CHUNK):
        chunk = value[at : at + CHUNK]
        high = chunk.astype(bf16)
        coarse = (chunk * 2.0**power_of).astype(f8)
        low = ((chunk - high.astype(f32)) * 2.0 ** (power_of + 8)).astype(f8)
        lines = slice(row + at, row + at + CHUNK)
        high_ref[lines, columns] = high
        left_ref[lines, columns] = coarse
        left_ref[lines, later] = low
        right_ref[lines, columns] = low
        right_ref[slice(size + row + at, size + row + at + CHUNK), columns] = coarse


def dot(left, right):
    return jnp.dot(left, right, preferred_element_type=f32)


def product(left, right, rows, columns, power_of):
    main = dot(left[0][rows, :], right[0][:, columns])
    return main + dot(left[1][rows, :], right[2][:, columns]) * 2.0 ** -(power_of + 8)


def polish_kernel(width, packed_ref, x_ref, merged_ref, out_ref, kept_ref, *scratch):
    gram_ref, half_ref, rest_ref, pair_ref, done = scratch[:5]
    gram_form, first_form, half_form, second_form, pair_form = (scratch[at : at + 3] for at in range(5, 20, 3))
    store = pltpu.make_async_copy(merged_ref, kept_ref, done)
    store.start()
    size = x_ref.shape[0]
    front, back = slice(0, size // 2), slice(size // 2, size)
    blocks = ((front, front), (front, back), (back, back))

    scale = power(packed_ref[:, 7:8, 0:1])
    row = lax.broadcasted_iota(jnp.int32, (TILE, TILE), 0)
    column = lax.broadcasted_iota(jnp.int32, (TILE, TILE), 1)
    pieces = [(at, r * TILE, s * TILE) for at, (r, s) in enumerate(upper(size // TILE))]
    load = lambda at, factor: (packed_ref[:, at * 8 : (at + 1) * 8, :] * factor).reshape(TILE, TILE)
    diagonal = [jnp.where(row == column, load(at, scale), 0.0) for at, r, s in pieces if r == s]
    total = jnp.sum(sum(diagonal), keepdims=True)
    inverse = 1.0 / (jnp.sqrt(total) + epsilon)
    factor = scale * (inverse * inverse).reshape(1, 1, 1)
    for at, r, s in pieces:
        block = load(at, factor)
        if r == s:
            block = jnp.where(row > column, block.T, block)
        gram_ref[r : r + TILE, s : s + TILE] = block
        put(gram_form, block, r, s, 7)
        if r != s:
            gram_ref[s : s + TILE, r : r + TILE] = block.T
            put(gram_form, block.T, s, r, 7)

    def symmetric(left, right, power_of, finish, form, form_power, kept=None):
        for rows, columns in blocks:
            value = finish(product(left, right, rows, columns, power_of), rows, columns)
            if kept is not None:
                kept[rows, columns] = value
            put(form, value, rows.start, columns.start, form_power)
            if rows != columns:
                put(form, value.T, columns.start, rows.start, form_power)

    def rest(step):
        def finish(square, rows, columns):
            value = coef_b * gram_ref[rows, columns] + coef_c * square
            if step == 0:
                rest_ref[rows, columns] = coef_a * value
            if step == 1:
                rest_ref[rows, columns] = rest_ref[rows, columns] + coef_a * value
            return value

        return finish

    def pair(value, rows, columns):
        value = rest_ref[rows, columns] + value
        if rows == columns:
            line = lax.broadcasted_iota(jnp.int32, value.shape, 0)
            value += jnp.where(line == lax.broadcasted_iota(jnp.int32, value.shape, 1), coef_a**2, 0.0)
        return value

    once = lambda value, rows, columns: coef_a * gram_ref[rows, columns] + value
    twice = lambda value, rows, columns: coef_a * half_ref[rows, columns] + value
    symmetric(gram_form, gram_form, 14, rest(0), first_form, 7)
    symmetric(gram_form, first_form, 14, once, half_form, 7, half_ref)
    symmetric(half_form, first_form, 14, twice, gram_form, 7, gram_ref)
    symmetric(gram_form, gram_form, 14, rest(1), second_form, 7)
    symmetric(gram_form, second_form, 14, once, half_form, 7, half_ref)
    symmetric(second_form, first_form, 14, pair, pair_form, 5, pair_ref)
    symmetric(half_form, second_form, 14, twice, gram_form, 7, gram_ref)
    symmetric(gram_form, gram_form, 14, rest(2), first_form, 7)
    near, across, far = (coef_a * pair_ref[r, c] + product(first_form, pair_form, r, c, 12) for r, c in blocks)
    x = x_ref[...]
    unit = (x.astype(f32) * (inverse * 2.0**8)).astype(f8)
    for rows, lines in ((front, (near, across)), (back, (across.T, far))):
        whole = jnp.concatenate(lines, axis=1)
        high = whole.astype(bf16)
        low = ((whole - high.astype(f32)) * 2.0**11).astype(f8)
        current = dot(high, x) * inverse + dot(low, unit) * 2.0**-19
        out_ref[rows] = (0.2 * math.sqrt(width) * current).astype(bf16)
    store.wait()


def keep_kernel(in_ref, out_ref, done):
    copy = pltpu.make_async_copy(in_ref, out_ref, done)
    copy.start()
    copy.wait()


def keep(value):
    return pl.pallas_call(
        keep_kernel,
        out_shape=jax.ShapeDtypeStruct(value.shape, value.dtype),
        in_specs=[pl.BlockSpec(memory_space=pl.ANY)],
        out_specs=pl.BlockSpec(memory_space=pltpu.HBM),
        scratch_shapes=[pltpu.SemaphoreType.DMA],
        compiler_params=pltpu.CompilerParams(vmem_limit_bytes=16 << 20),
    )(value)


def polish(start, merged, parts):
    rows, columns = start.shape
    vmem = pl.BlockSpec(memory_space=pltpu.VMEM)
    params = pltpu.CompilerParams(vmem_limit_bytes=48 << 20)
    share = (len(upper(rows // TILE)) * 8, TILE)
    packed = pl.pallas_call(
        gram_kernel,
        out_shape=jax.ShapeDtypeStruct((parts, *share), f32),
        in_specs=[vmem],
        out_specs=vmem,
        compiler_params=params,
    )(start)
    packed = packed.astype(jnp.float16)
    packed = lax.all_to_all(packed, "mp", split_axis=0, concat_axis=0, tiled=True)
    total = pl.pallas_call(
        sum_kernel,
        out_shape=jax.ShapeDtypeStruct(share, f32),
        in_specs=[vmem],
        out_specs=vmem,
        compiler_params=params,
    )(packed.astype(f32))
    copies = jnp.broadcast_to(total.astype(jnp.float16), (parts, *share))
    copies = lax.all_to_all(copies, "mp", split_axis=0, concat_axis=0, tiled=True)
    return pl.pallas_call(
        lambda *refs: polish_kernel(columns * parts, *refs),
        out_shape=(
            jax.ShapeDtypeStruct(start.shape, bf16),
            jax.ShapeDtypeStruct(merged.shape, f32),
        ),
        in_specs=[vmem] * 3,
        out_specs=(vmem, pl.BlockSpec(memory_space=pltpu.HBM)),
        scratch_shapes=[pltpu.VMEM((rows, rows), f32)] * 4
        + [pltpu.SemaphoreType.DMA]
        + [pltpu.VMEM((rows, rows), bf16), pltpu.VMEM((rows, 2 * rows), f8), pltpu.VMEM((2 * rows, rows), f8)] * 5,
        compiler_params=params,
    )(copies.astype(f32), start, merged)


def exchange(value):
    order = [device ^ 1 for device in range(value.shape[0])]
    return lax.all_to_all(value, "dp", split_axis=0, concat_axis=0, tiled=True, axis_index_groups=[order])


def body(grad, momentum, old_slot, new_slot):
    merged, start = merge(grad, momentum, old_slot, new_slot)
    got = exchange(start)
    slots, rows, columns = got.shape
    update, merged = polish(got.reshape(slots * rows, columns), merged, lax.axis_size("mp"))
    update = update.reshape(slots, rows, columns)
    return merged, keep(exchange(update))


def solution(mesh):
    placed = (P(None, "dp", "mp"), P(None, "dp", "mp"), P(), P())
    return jax.shard_map(
        body,
        mesh=mesh,
        in_specs=placed,
        out_specs=(P(None, "dp", "mp"), P(None, "dp", "mp")),
        check_vma=False,
    )
```

```python
import math

import jax
import jax.numpy as jnp
from jax import lax
from jax.experimental import pallas as pl
from jax.experimental.pallas import tpu as pltpu
from jax.sharding import PartitionSpec as P

coef_a = 3.4445
coef_b = -4.775
coef_c = 2.0315
beta = 0.95
epsilon = 1e-07
TILE = 128
bf16 = jnp.bfloat16
f32 = jnp.float32


def merge_kernel(
    old_ref, new_ref, grad_ref, mom_ref, merged_ref, start_ref, old, new, grad, mom, sems
):
    loads = [
        pltpu.make_async_copy(source, target, sems.at[at])
        for at, (source, target) in enumerate(
            [(mom_ref, mom), (grad_ref, grad), (old_ref, old), (new_ref, new)]
        )
    ]
    for load in loads:
        load.start()
    for load in loads:
        load.wait()
    for j in range(grad.shape[0]):
        slot = new[j]
        value = beta * mom[old[j]] + grad[slot].astype(f32)
        start_ref[slot] = value.astype(bf16)
        merged_ref[slot] = value


def merge(grad, momentum, old_slot, new_slot):
    hbm = pl.BlockSpec(memory_space=pltpu.HBM)
    return pl.pallas_call(
        merge_kernel,
        out_shape=(
            jax.ShapeDtypeStruct(momentum.shape, f32),
            jax.ShapeDtypeStruct(grad.shape, bf16),
        ),
        in_specs=[hbm] * 4,
        out_specs=(pl.BlockSpec(memory_space=pltpu.VMEM),) * 2,
        scratch_shapes=[
            pltpu.SMEM(old_slot.shape, jnp.int32),
            pltpu.SMEM(new_slot.shape, jnp.int32),
            pltpu.VMEM(grad.shape, bf16),
            pltpu.VMEM(momentum.shape, f32),
            pltpu.SemaphoreType.DMA((4,)),
        ],
        compiler_params=pltpu.CompilerParams(vmem_limit_bytes=32 << 20),
    )(*(pltpu.with_memory_space_constraint(x, pltpu.HBM) for x in (old_slot, new_slot, grad, momentum)))


def upper(count):
    return [(r, s) for r in range(count) for s in range(r, count)]


def exponent(bound):
    return jnp.floor(jnp.log(jnp.maximum(bound, 1e-30)) * (1.0 / math.log(2.0))) - 14.0


def power(value):
    return jnp.exp(value * math.log(2.0))


def spot(rows):
    row = lax.broadcasted_iota(jnp.int32, (rows, TILE), 0)
    return (row % 8 == 7) & (lax.broadcasted_iota(jnp.int32, (rows, TILE), 1) == 0)


def gram_kernel(x_ref, out_ref):
    x = x_ref[...]
    half = x.shape[0] // 2
    split = half // TILE
    dots = lambda p, q: lax.dot_general(p, q, (((1,), (1,)), ((), ())), preferred_element_type=f32)
    top, corner = dots(x[:half], x), dots(x[half:], x[half:])
    wide = x.astype(f32)
    bound = jnp.max(jnp.sum(wide * wide, axis=1, keepdims=True), axis=0, keepdims=True)
    power_of = exponent(bound)
    scale = power(-power_of)
    parts = out_ref.shape[0]
    for at, (r, s) in enumerate(upper(x.shape[0] // TILE)):
        gram, r, s = (top, r, s) if r < split else (corner, r - split, s - split)
        block = gram[r * TILE : (r + 1) * TILE, s * TILE : (s + 1) * TILE] * scale
        if at == 0:
            block = jnp.where(spot(TILE), power_of, block)
        out_ref[:, at * 8 : (at + 1) * 8, :] = block.reshape(parts, 8, TILE)


def sum_kernel(parts_ref, out_ref):
    powers = parts_ref[:, 7:8, 0:1]
    power_of = jnp.max(powers, axis=0) + math.ceil(math.log2(parts_ref.shape[0]))
    scales = power(powers - power_of)
    total = jnp.zeros(out_ref.shape, f32)
    for k in range(parts_ref.shape[0]):
        total += parts_ref[k] * scales[k]
    row = lax.broadcasted_iota(jnp.int32, out_ref.shape, 0)
    marks = (row == 7) & (lax.broadcasted_iota(jnp.int32, out_ref.shape, 1) == 0)
    out_ref[...] = jnp.where(marks, power_of, total)


def split(value):
    high = value.astype(bf16)
    return high, (value - high.astype(f32)).astype(bf16)


def dot(left, right):
    return jnp.dot(left, right, preferred_element_type=f32)


def product(left, right):
    (lh, ll), (rh, rl) = left, right
    return dot(jnp.concatenate([lh, ll, lh], axis=1), jnp.concatenate([rh, rh, rl], axis=0))


def symmetric(left, right):
    half = left[0].shape[0] // 2
    top = product([p[:half] for p in left], right)
    corner = product([p[half:] for p in left], [p[:, half:] for p in right])
    return jnp.concatenate([top, jnp.concatenate([top[:, half:].T, corner], axis=1)], axis=0)


def polish_kernel(width, packed_ref, x_ref, merged_ref, out_ref, kept_ref, gram_ref, done):
    store = pltpu.make_async_copy(merged_ref, kept_ref, done)
    store.start()
    rows = x_ref.shape[0]
    parts = packed_ref.shape[0]
    scale = power(packed_ref[:, 7:8, 0:1])
    row = lax.broadcasted_iota(jnp.int32, (TILE, TILE), 0)
    column = lax.broadcasted_iota(jnp.int32, (TILE, TILE), 1)
    pieces = [(at, r * TILE, s * TILE) for at, (r, s) in enumerate(upper(rows // TILE))]
    load = lambda at, factor: (packed_ref[:, at * 8 : (at + 1) * 8, :] * factor).reshape(TILE, TILE)
    traces = [jnp.where(row == column, load(at, scale), 0.0) for at, r, s in pieces if r == s]
    total = jnp.sum(sum(traces), keepdims=True)
    inverse = 1.0 / (jnp.sqrt(total) + epsilon)
    factor = scale * (inverse * inverse).reshape(1, 1, 1)
    for at, r, s in pieces:
        block = load(at, factor)
        if r == s:
            block = jnp.where(row > column, block.T, block)
        gram_ref[r : r + TILE, s : s + TILE] = block
        if r != s:
            gram_ref[s : s + TILE, r : r + TILE] = block.T
    gram = gram_ref[...]
    row = lax.broadcasted_iota(jnp.int32, (rows, rows), 0)
    diagonal = row == lax.broadcasted_iota(jnp.int32, (rows, rows), 1)
    rests, steps = [], []
    for step in range(3):
        g = split(gram)
        rest = coef_b * gram + coef_c * symmetric(g, g)
        q = split(rest)
        rests.append(rest)
        steps.append(q)
        if step < 2:
            half = coef_a * gram + symmetric(g, q)
        if step == 1:
            both = coef_a * (rests[0] + rests[1]) + symmetric(q, steps[0])
            both += jnp.where(diagonal, coef_a * coef_a, 0.0)
        if step < 2:
            gram = coef_a * half + symmetric(split(half), q)
    whole = split(coef_a * both + symmetric(steps[2], split(both)))
    x = x_ref[...]
    current = dot(whole[0], x) + dot(whole[1], x)
    out_ref[...] = (0.2 * math.sqrt(width) * inverse * current).astype(bf16)
    store.wait()


def keep_kernel(in_ref, out_ref, done):
    copy = pltpu.make_async_copy(in_ref, out_ref, done)
    copy.start()
    copy.wait()


def keep(value):
    return pl.pallas_call(
        keep_kernel,
        out_shape=jax.ShapeDtypeStruct(value.shape, value.dtype),
        in_specs=[pl.BlockSpec(memory_space=pl.ANY)],
        out_specs=pl.BlockSpec(memory_space=pltpu.HBM),
        scratch_shapes=[pltpu.SemaphoreType.DMA],
        compiler_params=pltpu.CompilerParams(vmem_limit_bytes=16 << 20),
    )(value)


def polish(start, merged, parts):
    rows, columns = start.shape
    vmem = pl.BlockSpec(memory_space=pltpu.VMEM)
    params = pltpu.CompilerParams(vmem_limit_bytes=48 << 20)
    share = (len(upper(rows // TILE)) * 8, TILE)
    packed = pl.pallas_call(
        gram_kernel,
        out_shape=jax.ShapeDtypeStruct((parts, *share), f32),
        in_specs=[vmem],
        out_specs=vmem,
        compiler_params=params,
    )(start)
    packed = packed.astype(jnp.float16)
    packed = lax.all_to_all(packed, "mp", split_axis=0, concat_axis=0, tiled=True)
    total = pl.pallas_call(
        sum_kernel,
        out_shape=jax.ShapeDtypeStruct(share, f32),
        in_specs=[vmem],
        out_specs=vmem,
        compiler_params=params,
    )(packed.astype(f32))
    copies = jnp.broadcast_to(total.astype(jnp.float16), (parts, *share))
    copies = lax.all_to_all(copies, "mp", split_axis=0, concat_axis=0, tiled=True)
    return pl.pallas_call(
        lambda *refs: polish_kernel(columns * parts, *refs),
        out_shape=(
            jax.ShapeDtypeStruct(start.shape, bf16),
            jax.ShapeDtypeStruct(merged.shape, f32),
        ),
        in_specs=[vmem] * 3,
        out_specs=(vmem, pl.BlockSpec(memory_space=pltpu.HBM)),
        scratch_shapes=[pltpu.VMEM((rows, rows), f32), pltpu.SemaphoreType.DMA],
        compiler_params=params,
    )(copies.astype(f32), start, merged)


def exchange(value):
    order = [device ^ 1 for device in range(value.shape[0])]
    return lax.all_to_all(value, "dp", split_axis=0, concat_axis=0, tiled=True, axis_index_groups=[order])


def body(grad, momentum, old_slot, new_slot):
    merged, start = merge(grad, momentum, old_slot, new_slot)
    got = exchange(start)
    slots, rows, columns = got.shape
    update, merged = polish(got.reshape(slots * rows, columns), merged, lax.axis_size("mp"))
    update = update.reshape(slots, rows, columns)
    return merged, keep(exchange(update))


def solution(mesh):
    placed = (P(None, "dp", "mp"), P(None, "dp", "mp"), P(), P())
    return jax.shard_map(
        body,
        mesh=mesh,
        in_specs=placed,
        out_specs=(P(None, "dp", "mp"), P(None, "dp", "mp")),
        check_vma=False,
    )
```

```python
import math

import jax
import jax.numpy as jnp
from jax import lax
from jax.experimental import pallas as pl
from jax.experimental.pallas import tpu as pltpu
from jax.sharding import PartitionSpec as P

coef_a = 3.4445
coef_b = -4.775
coef_c = 2.0315
beta = 0.95
epsilon = 1e-07
TILE = 128
bf16 = jnp.bfloat16
f32 = jnp.float32


def merge_kernel(
    old_ref, new_ref, grad_ref, mom_ref, merged_ref, start_ref, old, new, grad, mom, sems
):
    loads = [
        pltpu.make_async_copy(source, target, sems.at[at])
        for at, (source, target) in enumerate(
            [(mom_ref, mom), (grad_ref, grad), (old_ref, old), (new_ref, new)]
        )
    ]
    for load in loads:
        load.start()
    for load in loads:
        load.wait()
    for j in range(grad.shape[0]):
        slot = new[j]
        value = beta * mom[old[j]] + grad[slot].astype(f32)
        start_ref[slot] = value.astype(bf16)
        merged_ref[slot] = value


def merge(grad, momentum, old_slot, new_slot):
    hbm = pl.BlockSpec(memory_space=pltpu.HBM)
    return pl.pallas_call(
        merge_kernel,
        out_shape=(
            jax.ShapeDtypeStruct(momentum.shape, f32),
            jax.ShapeDtypeStruct(grad.shape, bf16),
        ),
        in_specs=[hbm] * 4,
        out_specs=(pl.BlockSpec(memory_space=pltpu.VMEM),) * 2,
        scratch_shapes=[
            pltpu.SMEM(old_slot.shape, jnp.int32),
            pltpu.SMEM(new_slot.shape, jnp.int32),
            pltpu.VMEM(grad.shape, bf16),
            pltpu.VMEM(momentum.shape, f32),
            pltpu.SemaphoreType.DMA((4,)),
        ],
        compiler_params=pltpu.CompilerParams(vmem_limit_bytes=32 << 20),
    )(*(pltpu.with_memory_space_constraint(x, pltpu.HBM) for x in (old_slot, new_slot, grad, momentum)))


def upper(count):
    return [(r, s) for r in range(count) for s in range(r, count)]


def exponent(bound):
    return jnp.floor(jnp.log(jnp.maximum(bound, 1e-30)) * (1.0 / math.log(2.0))) - 14.0


def power(value):
    return jnp.exp(value * math.log(2.0))


def spot(rows):
    row = lax.broadcasted_iota(jnp.int32, (rows, TILE), 0)
    return (row % 8 == 7) & (lax.broadcasted_iota(jnp.int32, (rows, TILE), 1) == 0)


def gram_kernel(x_ref, out_ref):
    x = x_ref[...]
    half = x.shape[0] // 2
    split = half // TILE
    dots = lambda p, q: lax.dot_general(p, q, (((1,), (1,)), ((), ())), preferred_element_type=f32)
    top, corner = dots(x[:half], x), dots(x[half:], x[half:])
    wide = x.astype(f32)
    bound = jnp.max(jnp.sum(wide * wide, axis=1, keepdims=True), axis=0, keepdims=True)
    power_of = exponent(bound)
    scale = power(-power_of)
    parts = out_ref.shape[0]
    for at, (r, s) in enumerate(upper(x.shape[0] // TILE)):
        gram, r, s = (top, r, s) if r < split else (corner, r - split, s - split)
        block = gram[r * TILE : (r + 1) * TILE, s * TILE : (s + 1) * TILE] * scale
        if at == 0:
            block = jnp.where(spot(TILE), power_of, block)
        out_ref[:, at * 8 : (at + 1) * 8, :] = block.reshape(parts, 8, TILE)


def sum_kernel(parts_ref, out_ref):
    powers = parts_ref[:, 7:8, 0:1]
    power_of = jnp.max(powers, axis=0) + math.ceil(math.log2(parts_ref.shape[0]))
    scales = power(powers - power_of)
    total = jnp.zeros(out_ref.shape, f32)
    for k in range(parts_ref.shape[0]):
        total += parts_ref[k] * scales[k]
    row = lax.broadcasted_iota(jnp.int32, out_ref.shape, 0)
    marks = (row == 7) & (lax.broadcasted_iota(jnp.int32, out_ref.shape, 1) == 0)
    out_ref[...] = jnp.where(marks, power_of, total)


def split(value):
    high = value.astype(bf16)
    return high, (value - high.astype(f32)).astype(bf16)


def dot(left, right):
    return jnp.dot(left, right, preferred_element_type=f32)


def product(left, right):
    (lh, ll), (rh, rl) = left, right
    return dot(jnp.concatenate([lh, ll, lh], axis=1), jnp.concatenate([rh, rh, rl], axis=0))


def symmetric(left, right):
    half = left[0].shape[0] // 2
    top = product([p[:half] for p in left], right)
    corner = product([p[half:] for p in left], [p[:, half:] for p in right])
    return jnp.concatenate([top, jnp.concatenate([top[:, half:].T, corner], axis=1)], axis=0)


def polish_kernel(width, packed_ref, x_ref, merged_ref, out_ref, kept_ref, gram_ref, done):
    store = pltpu.make_async_copy(merged_ref, kept_ref, done)
    store.start()
    rows = x_ref.shape[0]
    parts = packed_ref.shape[0]
    scale = power(packed_ref[:, 7:8, 0:1])
    row = lax.broadcasted_iota(jnp.int32, (TILE, TILE), 0)
    column = lax.broadcasted_iota(jnp.int32, (TILE, TILE), 1)
    pieces = [(at, r * TILE, s * TILE) for at, (r, s) in enumerate(upper(rows // TILE))]
    load = lambda at, factor: (packed_ref[:, at * 8 : (at + 1) * 8, :] * factor).reshape(TILE, TILE)
    traces = [jnp.where(row == column, load(at, scale), 0.0) for at, r, s in pieces if r == s]
    total = jnp.sum(sum(traces), keepdims=True)
    inverse = 1.0 / (jnp.sqrt(total) + epsilon)
    factor = scale * (inverse * inverse).reshape(1, 1, 1)
    for at, r, s in pieces:
        block = load(at, factor)
        if r == s:
            block = jnp.where(row > column, block.T, block)
        gram_ref[r : r + TILE, s : s + TILE] = block
        if r != s:
            gram_ref[s : s + TILE, r : r + TILE] = block.T
    gram = gram_ref[...]
    row = lax.broadcasted_iota(jnp.int32, (rows, rows), 0)
    diagonal = row == lax.broadcasted_iota(jnp.int32, (rows, rows), 1)
    rests, steps = [], []
    for step in range(3):
        g = split(gram)
        rest = coef_b * gram + coef_c * symmetric(g, g)
        q = split(rest)
        rests.append(rest)
        steps.append(q)
        if step < 2:
            half = coef_a * gram + symmetric(g, q)
        if step == 1:
            both = coef_a * (rests[0] + rests[1]) + symmetric(q, steps[0])
            both += jnp.where(diagonal, coef_a * coef_a, 0.0)
        if step < 2:
            gram = coef_a * half + symmetric(split(half), q)
    whole = split(coef_a * both + symmetric(steps[2], split(both)))
    x = x_ref[...]
    current = dot(whole[0], x) + dot(whole[1], x)
    out_ref[...] = (0.2 * math.sqrt(width) * inverse * current).astype(bf16)
    store.wait()


def keep_kernel(in_ref, out_ref, done):
    copy = pltpu.make_async_copy(in_ref, out_ref, done)
    copy.start()
    copy.wait()


def keep(value):
    return pl.pallas_call(
        keep_kernel,
        out_shape=jax.ShapeDtypeStruct(value.shape, value.dtype),
        in_specs=[pl.BlockSpec(memory_space=pl.ANY)],
        out_specs=pl.BlockSpec(memory_space=pltpu.HBM),
        scratch_shapes=[pltpu.SemaphoreType.DMA],
        compiler_params=pltpu.CompilerParams(vmem_limit_bytes=16 << 20),
    )(value)


def share_out(value):
    side = math.isqrt(value.shape[0])
    turn = [(at + side // 2) % side for at in range(side)]
    order = [side * y + x for y in turn for x in turn]
    return lax.all_to_all(value, "mp", split_axis=0, concat_axis=0, tiled=True, axis_index_groups=[order])


def polish(start, merged, parts):
    rows, columns = start.shape
    vmem = pl.BlockSpec(memory_space=pltpu.VMEM)
    params = pltpu.CompilerParams(vmem_limit_bytes=48 << 20)
    share = (len(upper(rows // TILE)) * 8, TILE)
    packed = pl.pallas_call(
        gram_kernel,
        out_shape=jax.ShapeDtypeStruct((parts, *share), f32),
        in_specs=[vmem],
        out_specs=vmem,
        compiler_params=params,
    )(start)
    packed = packed.astype(jnp.float16)
    packed = share_out(packed)
    total = pl.pallas_call(
        sum_kernel,
        out_shape=jax.ShapeDtypeStruct(share, f32),
        in_specs=[vmem],
        out_specs=vmem,
        compiler_params=params,
    )(packed.astype(f32))
    copies = jnp.broadcast_to(total.astype(jnp.float16), (parts, *share))
    copies = share_out(copies)
    return pl.pallas_call(
        lambda *refs: polish_kernel(columns * parts, *refs),
        out_shape=(
            jax.ShapeDtypeStruct(start.shape, bf16),
            jax.ShapeDtypeStruct(merged.shape, f32),
        ),
        in_specs=[vmem] * 3,
        out_specs=(vmem, pl.BlockSpec(memory_space=pltpu.HBM)),
        scratch_shapes=[pltpu.VMEM((rows, rows), f32), pltpu.SemaphoreType.DMA],
        compiler_params=params,
    )(copies.astype(f32), start, merged)


def exchange(value):
    order = [device ^ 1 for device in range(value.shape[0])]
    return lax.all_to_all(value, "dp", split_axis=0, concat_axis=0, tiled=True, axis_index_groups=[order])


def body(grad, momentum, old_slot, new_slot):
    merged, start = merge(grad, momentum, old_slot, new_slot)
    got = exchange(start)
    slots, rows, columns = got.shape
    update, merged = polish(got.reshape(slots * rows, columns), merged, lax.axis_size("mp"))
    update = update.reshape(slots, rows, columns)
    return merged, keep(exchange(update))


def solution(mesh):
    placed = (P(None, "dp", "mp"), P(None, "dp", "mp"), P(), P())
    return jax.shard_map(
        body,
        mesh=mesh,
        in_specs=placed,
        out_specs=(P(None, "dp", "mp"), P(None, "dp", "mp")),
        check_vma=False,
    )
```

```python
import math

import jax
import jax.numpy as jnp
from jax import lax
from jax.experimental import pallas as pl
from jax.experimental.pallas import tpu as pltpu
from jax.sharding import PartitionSpec as P

coef_a = 3.4445
coef_b = -4.775
coef_c = 2.0315
beta = 0.95
epsilon = 1e-07
TILE = 128
bf16 = jnp.bfloat16
f32 = jnp.float32


def merge_kernel(
    old_ref, new_ref, grad_ref, mom_ref, merged_ref, start_ref, old, new, grad, mom, sems
):
    loads = [
        pltpu.make_async_copy(source, target, sems.at[at])
        for at, (source, target) in enumerate(
            [(mom_ref, mom), (grad_ref, grad), (old_ref, old), (new_ref, new)]
        )
    ]
    for load in loads:
        load.start()
    for load in loads:
        load.wait()
    for j in range(grad.shape[0]):
        slot = new[j]
        value = beta * mom[old[j]] + grad[slot].astype(f32)
        start_ref[slot] = value.astype(bf16)
        merged_ref[slot] = value


def merge(grad, momentum, old_slot, new_slot):
    hbm = pl.BlockSpec(memory_space=pltpu.HBM)
    return pl.pallas_call(
        merge_kernel,
        out_shape=(
            jax.ShapeDtypeStruct(momentum.shape, f32),
            jax.ShapeDtypeStruct(grad.shape, bf16),
        ),
        in_specs=[hbm] * 4,
        out_specs=(pl.BlockSpec(memory_space=pltpu.VMEM),) * 2,
        scratch_shapes=[
            pltpu.SMEM(old_slot.shape, jnp.int32),
            pltpu.SMEM(new_slot.shape, jnp.int32),
            pltpu.VMEM(grad.shape, bf16),
            pltpu.VMEM(momentum.shape, f32),
            pltpu.SemaphoreType.DMA((4,)),
        ],
        compiler_params=pltpu.CompilerParams(vmem_limit_bytes=32 << 20),
    )(*(pltpu.with_memory_space_constraint(x, pltpu.HBM) for x in (old_slot, new_slot, grad, momentum)))


def upper(count):
    return [(r, s) for r in range(count) for s in range(r, count)]


def exponent(bound):
    return jnp.floor(jnp.log(jnp.maximum(bound, 1e-30)) * (1.0 / math.log(2.0))) - 14.0


def power(value):
    return jnp.exp(value * math.log(2.0))


def spot(rows):
    row = lax.broadcasted_iota(jnp.int32, (rows, TILE), 0)
    return (row % 8 == 7) & (lax.broadcasted_iota(jnp.int32, (rows, TILE), 1) == 0)


def gram_kernel(x_ref, out_ref):
    x = x_ref[...]
    half = x.shape[0] // 2
    split = half // TILE
    dots = lambda p, q: lax.dot_general(p, q, (((1,), (1,)), ((), ())), preferred_element_type=f32)
    top, corner = dots(x[:half], x), dots(x[half:], x[half:])
    wide = x.astype(f32)
    bound = jnp.max(jnp.sum(wide * wide, axis=1, keepdims=True), axis=0, keepdims=True)
    power_of = exponent(bound)
    scale = power(-power_of)
    parts = out_ref.shape[0]
    for at, (r, s) in enumerate(upper(x.shape[0] // TILE)):
        gram, r, s = (top, r, s) if r < split else (corner, r - split, s - split)
        block = gram[r * TILE : (r + 1) * TILE, s * TILE : (s + 1) * TILE] * scale
        if at == 0:
            block = jnp.where(spot(TILE), power_of, block)
        out_ref[:, at * 8 : (at + 1) * 8, :] = block.reshape(parts, 8, TILE)


def sum_kernel(parts_ref, out_ref):
    powers = parts_ref[:, 7:8, 0:1]
    power_of = jnp.max(powers, axis=0) + math.ceil(math.log2(parts_ref.shape[0]))
    scales = power(powers - power_of)
    total = jnp.zeros(out_ref.shape, f32)
    for k in range(parts_ref.shape[0]):
        total += parts_ref[k] * scales[k]
    row = lax.broadcasted_iota(jnp.int32, out_ref.shape, 0)
    marks = (row == 7) & (lax.broadcasted_iota(jnp.int32, out_ref.shape, 1) == 0)
    out_ref[...] = jnp.where(marks, power_of, total)


def split(value):
    high = value.astype(bf16)
    return high, (value - high.astype(f32)).astype(bf16)


def dot(left, right):
    return jnp.dot(left, right, preferred_element_type=f32)


def product(left, right):
    (lh, ll), (rh, rl) = left, right
    return dot(jnp.concatenate([lh, ll, lh], axis=1), jnp.concatenate([rh, rh, rl], axis=0))


def symmetric(left, right):
    half = left[0].shape[0] // 2
    top = product([p[:half] for p in left], right)
    corner = product([p[half:] for p in left], [p[:, half:] for p in right])
    return jnp.concatenate([top, jnp.concatenate([top[:, half:].T, corner], axis=1)], axis=0)


def polish_kernel(width, packed_ref, x_ref, merged_ref, out_ref, kept_ref, gram_ref, done):
    store = pltpu.make_async_copy(merged_ref, kept_ref, done)
    store.start()
    rows = x_ref.shape[0]
    parts = packed_ref.shape[0]
    scale = power(packed_ref[:, 7:8, 0:1])
    row = lax.broadcasted_iota(jnp.int32, (TILE, TILE), 0)
    column = lax.broadcasted_iota(jnp.int32, (TILE, TILE), 1)
    pieces = [(at, r * TILE, s * TILE) for at, (r, s) in enumerate(upper(rows // TILE))]
    load = lambda at, factor: (packed_ref[:, at * 8 : (at + 1) * 8, :] * factor).reshape(TILE, TILE)
    traces = [jnp.where(row == column, load(at, scale), 0.0) for at, r, s in pieces if r == s]
    total = jnp.sum(sum(traces), keepdims=True)
    inverse = 1.0 / (jnp.sqrt(total) + epsilon)
    factor = scale * (inverse * inverse).reshape(1, 1, 1)
    for at, r, s in pieces:
        block = load(at, factor)
        if r == s:
            block = jnp.where(row > column, block.T, block)
        gram_ref[r : r + TILE, s : s + TILE] = block
        if r != s:
            gram_ref[s : s + TILE, r : r + TILE] = block.T
    gram = gram_ref[...]
    row = lax.broadcasted_iota(jnp.int32, (rows, rows), 0)
    diagonal = row == lax.broadcasted_iota(jnp.int32, (rows, rows), 1)
    rests, steps = [], []
    for step in range(3):
        g = split(gram)
        rest = coef_b * gram + coef_c * symmetric(g, g)
        q = split(rest)
        rests.append(rest)
        steps.append(q)
        if step < 2:
            half = coef_a * gram + symmetric(g, q)
        if step == 1:
            both = coef_a * (rests[0] + rests[1]) + symmetric(q, steps[0])
            both += jnp.where(diagonal, coef_a * coef_a, 0.0)
        if step < 2:
            gram = coef_a * half + symmetric(split(half), q)
    whole = split(coef_a * both + symmetric(steps[2], split(both)))
    x = x_ref[...]
    current = dot(whole[0], x) + dot(whole[1], x)
    out_ref[...] = (0.2 * math.sqrt(width) * inverse * current).astype(bf16)
    store.wait()


def keep_kernel(in_ref, out_ref, done):
    copy = pltpu.make_async_copy(in_ref, out_ref, done)
    copy.start()
    copy.wait()


def keep(value):
    return pl.pallas_call(
        keep_kernel,
        out_shape=jax.ShapeDtypeStruct(value.shape, value.dtype),
        in_specs=[pl.BlockSpec(memory_space=pl.ANY)],
        out_specs=pl.BlockSpec(memory_space=pltpu.HBM),
        scratch_shapes=[pltpu.SemaphoreType.DMA],
        compiler_params=pltpu.CompilerParams(vmem_limit_bytes=16 << 20),
    )(value)


def share_out(value):
    side = math.isqrt(value.shape[0])
    turn = [(at + side // 2) % side for at in range(side)]
    order = [side * y + x for y in turn for x in turn]
    return lax.all_to_all(value, "mp", split_axis=0, concat_axis=0, tiled=True, axis_index_groups=[order])


def polish(start, merged, parts):
    rows, columns = start.shape
    vmem = pl.BlockSpec(memory_space=pltpu.VMEM)
    params = pltpu.CompilerParams(vmem_limit_bytes=48 << 20)
    share = (len(upper(rows // TILE)) * 8, TILE)
    packed = pl.pallas_call(
        gram_kernel,
        out_shape=jax.ShapeDtypeStruct((parts, *share), f32),
        in_specs=[vmem],
        out_specs=vmem,
        compiler_params=params,
    )(start)
    packed = packed.astype(jnp.float16)
    packed = share_out(packed)
    total = pl.pallas_call(
        sum_kernel,
        out_shape=jax.ShapeDtypeStruct(share, f32),
        in_specs=[vmem],
        out_specs=vmem,
        compiler_params=params,
    )(packed.astype(f32))
    copies = jnp.broadcast_to(total.astype(jnp.float16), (parts, *share))
    copies = share_out(copies)
    return pl.pallas_call(
        lambda *refs: polish_kernel(columns * parts, *refs),
        out_shape=(
            jax.ShapeDtypeStruct(start.shape, bf16),
            jax.ShapeDtypeStruct(merged.shape, f32),
        ),
        in_specs=[vmem] * 3,
        out_specs=(vmem, pl.BlockSpec(memory_space=pltpu.HBM)),
        scratch_shapes=[pltpu.VMEM((rows, rows), f32), pltpu.SemaphoreType.DMA],
        compiler_params=params,
    )(copies.astype(f32), start, merged)


def exchange(value):
    count = value.shape[0]
    order = [(device + count // 2) % count ^ 1 for device in range(count)]
    return lax.all_to_all(value, "dp", split_axis=0, concat_axis=0, tiled=True, axis_index_groups=[order])


def body(grad, momentum, old_slot, new_slot):
    merged, start = merge(grad, momentum, old_slot, new_slot)
    got = exchange(start)
    slots, rows, columns = got.shape
    update, merged = polish(got.reshape(slots * rows, columns), merged, lax.axis_size("mp"))
    update = update.reshape(slots, rows, columns)
    return merged, keep(exchange(update))


def solution(mesh):
    placed = (P(None, "dp", "mp"), P(None, "dp", "mp"), P(), P())
    return jax.shard_map(
        body,
        mesh=mesh,
        in_specs=placed,
        out_specs=(P(None, "dp", "mp"), P(None, "dp", "mp")),
        check_vma=False,
    )
```

```python
import math

import jax
import jax.numpy as jnp
from jax import lax
from jax.experimental import pallas as pl
from jax.experimental.pallas import tpu as pltpu
from jax.sharding import PartitionSpec as P

coef_a = 3.4445
coef_b = -4.775
coef_c = 2.0315
beta = 0.95
epsilon = 1e-07
TILE = 128
bf16 = jnp.bfloat16
f32 = jnp.float32


def merge_kernel(
    old_ref, new_ref, grad_ref, mom_ref, merged_ref, start_ref, old, new, grad, mom, sems
):
    loads = [
        pltpu.make_async_copy(source, target, sems.at[at])
        for at, (source, target) in enumerate(
            [(mom_ref, mom), (grad_ref, grad), (old_ref, old), (new_ref, new)]
        )
    ]
    for load in loads:
        load.start()
    for load in loads:
        load.wait()
    for j in range(grad.shape[0]):
        slot = new[j]
        value = beta * mom[old[j]] + grad[slot].astype(f32)
        start_ref[slot] = value.astype(bf16)
        merged_ref[slot] = value


def merge(grad, momentum, old_slot, new_slot):
    hbm = pl.BlockSpec(memory_space=pltpu.HBM)
    return pl.pallas_call(
        merge_kernel,
        out_shape=(
            jax.ShapeDtypeStruct(momentum.shape, f32),
            jax.ShapeDtypeStruct(grad.shape, bf16),
        ),
        in_specs=[hbm] * 4,
        out_specs=(pl.BlockSpec(memory_space=pltpu.VMEM),) * 2,
        scratch_shapes=[
            pltpu.SMEM(old_slot.shape, jnp.int32),
            pltpu.SMEM(new_slot.shape, jnp.int32),
            pltpu.VMEM(grad.shape, bf16),
            pltpu.VMEM(momentum.shape, f32),
            pltpu.SemaphoreType.DMA((4,)),
        ],
        compiler_params=pltpu.CompilerParams(vmem_limit_bytes=32 << 20),
    )(*(pltpu.with_memory_space_constraint(x, pltpu.HBM) for x in (old_slot, new_slot, grad, momentum)))


def upper(count):
    return [(r, s) for r in range(count) for s in range(r, count)]


def exponent(bound):
    return jnp.floor(jnp.log(jnp.maximum(bound, 1e-30)) * (1.0 / math.log(2.0))) - 14.0


def power(value):
    return jnp.exp(value * math.log(2.0))


def spot(rows):
    row = lax.broadcasted_iota(jnp.int32, (rows, TILE), 0)
    return (row % 8 == 7) & (lax.broadcasted_iota(jnp.int32, (rows, TILE), 1) == 0)


def gram_kernel(x_ref, out_ref):
    x = x_ref[...]
    half = x.shape[0] // 2
    split = half // TILE
    dots = lambda p, q: lax.dot_general(p, q, (((1,), (1,)), ((), ())), preferred_element_type=f32)
    top, corner = dots(x[:half], x), dots(x[half:], x[half:])
    wide = x.astype(f32)
    bound = jnp.max(jnp.sum(wide * wide, axis=1, keepdims=True), axis=0, keepdims=True)
    power_of = exponent(bound)
    scale = power(-power_of)
    parts = out_ref.shape[0]
    for at, (r, s) in enumerate(upper(x.shape[0] // TILE)):
        gram, r, s = (top, r, s) if r < split else (corner, r - split, s - split)
        block = gram[r * TILE : (r + 1) * TILE, s * TILE : (s + 1) * TILE] * scale
        if at == 0:
            block = jnp.where(spot(TILE), power_of, block)
        out_ref[:, at * 8 : (at + 1) * 8, :] = block.reshape(parts, 8, TILE)


def sum_kernel(parts_ref, out_ref):
    powers = parts_ref[:, 7:8, 0:1]
    power_of = jnp.max(powers, axis=0) + math.ceil(math.log2(parts_ref.shape[0]))
    scales = power(powers - power_of)
    total = jnp.zeros(out_ref.shape, f32)
    for k in range(parts_ref.shape[0]):
        total += parts_ref[k] * scales[k]
    row = lax.broadcasted_iota(jnp.int32, out_ref.shape, 0)
    marks = (row == 7) & (lax.broadcasted_iota(jnp.int32, out_ref.shape, 1) == 0)
    out_ref[...] = jnp.where(marks, power_of, total)


def split(value):
    high = value.astype(bf16)
    return high, (value - high.astype(f32)).astype(bf16)


def dot(left, right):
    return jnp.dot(left, right, preferred_element_type=f32)


def product(left, right):
    (lh, ll), (rh, rl) = left, right
    return dot(jnp.concatenate([lh, ll, lh], axis=1), jnp.concatenate([rh, rh, rl], axis=0))


def symmetric(left, right):
    half = left[0].shape[0] // 2
    top = product([p[:half] for p in left], right)
    corner = product([p[half:] for p in left], [p[:, half:] for p in right])
    return jnp.concatenate([top, jnp.concatenate([top[:, half:].T, corner], axis=1)], axis=0)


def polish_kernel(width, packed_ref, x_ref, merged_ref, out_ref, kept_ref, gram_ref, done):
    store = pltpu.make_async_copy(merged_ref, kept_ref, done)
    store.start()
    rows = x_ref.shape[0]
    parts = packed_ref.shape[0]
    scale = power(packed_ref[:, 7:8, 0:1])
    row = lax.broadcasted_iota(jnp.int32, (TILE, TILE), 0)
    column = lax.broadcasted_iota(jnp.int32, (TILE, TILE), 1)
    pieces = [(at, r * TILE, s * TILE) for at, (r, s) in enumerate(upper(rows // TILE))]
    load = lambda at, factor: (packed_ref[:, at * 8 : (at + 1) * 8, :] * factor).reshape(TILE, TILE)
    traces = [jnp.where(row == column, load(at, scale), 0.0) for at, r, s in pieces if r == s]
    total = jnp.sum(sum(traces), keepdims=True)
    inverse = 1.0 / (jnp.sqrt(total) + epsilon)
    factor = scale * (inverse * inverse).reshape(1, 1, 1)
    for at, r, s in pieces:
        block = load(at, factor)
        if r == s:
            block = jnp.where(row > column, block.T, block)
        gram_ref[r : r + TILE, s : s + TILE] = block
        if r != s:
            gram_ref[s : s + TILE, r : r + TILE] = block.T
    gram = gram_ref[...]
    row = lax.broadcasted_iota(jnp.int32, (rows, rows), 0)
    diagonal = row == lax.broadcasted_iota(jnp.int32, (rows, rows), 1)
    rests, steps = [], []
    for step in range(3):
        g = split(gram)
        rest = coef_b * gram + coef_c * symmetric(g, g)
        q = split(rest)
        rests.append(rest)
        steps.append(q)
        if step < 2:
            half = coef_a * gram + symmetric(g, q)
        if step == 1:
            both = coef_a * (rests[0] + rests[1]) + symmetric(q, steps[0])
            both += jnp.where(diagonal, coef_a * coef_a, 0.0)
        if step < 2:
            gram = coef_a * half + symmetric(split(half), q)
    whole = split(coef_a * both + symmetric(steps[2], split(both)))
    x = x_ref[...]
    current = dot(whole[0], x) + dot(whole[1], x)
    out_ref[...] = (0.2 * math.sqrt(width) * inverse * current).astype(bf16)
    store.wait()


def keep_kernel(in_ref, out_ref, done):
    copy = pltpu.make_async_copy(in_ref, out_ref, done)
    copy.start()
    copy.wait()


def keep(value):
    return pl.pallas_call(
        keep_kernel,
        out_shape=jax.ShapeDtypeStruct(value.shape, value.dtype),
        in_specs=[pl.BlockSpec(memory_space=pl.ANY)],
        out_specs=pl.BlockSpec(memory_space=pltpu.HBM),
        scratch_shapes=[pltpu.SemaphoreType.DMA],
        compiler_params=pltpu.CompilerParams(vmem_limit_bytes=16 << 20),
    )(value)


def share_out(value):
    side = math.isqrt(value.shape[0])
    turn = [(at + side // 2) % side for at in range(side)]
    order = [side * y + x for y in turn for x in turn]
    return lax.all_to_all(value, "mp", split_axis=0, concat_axis=0, tiled=True, axis_index_groups=[order])


def polish(start, merged, parts):
    rows, columns = start.shape
    vmem = pl.BlockSpec(memory_space=pltpu.VMEM)
    params = pltpu.CompilerParams(vmem_limit_bytes=48 << 20)
    share = (len(upper(rows // TILE)) * 8, TILE)
    packed = pl.pallas_call(
        gram_kernel,
        out_shape=jax.ShapeDtypeStruct((parts, *share), f32),
        in_specs=[vmem],
        out_specs=vmem,
        compiler_params=params,
    )(start)
    packed = packed.astype(jnp.float16)
    packed = share_out(packed)
    total = pl.pallas_call(
        sum_kernel,
        out_shape=jax.ShapeDtypeStruct(share, f32),
        in_specs=[vmem],
        out_specs=vmem,
        compiler_params=params,
    )(packed.astype(f32))
    copies = jnp.broadcast_to(total.astype(jnp.float16), (parts, *share))
    copies = share_out(copies)
    return pl.pallas_call(
        lambda *refs: polish_kernel(columns * parts, *refs),
        out_shape=(
            jax.ShapeDtypeStruct(start.shape, bf16),
            jax.ShapeDtypeStruct(merged.shape, f32),
        ),
        in_specs=[vmem] * 3,
        out_specs=(vmem, pl.BlockSpec(memory_space=pltpu.HBM)),
        scratch_shapes=[pltpu.VMEM((rows, rows), f32), pltpu.SemaphoreType.DMA],
        compiler_params=params,
    )(copies.astype(f32), start, merged)


def exchange(value):
    chips = value.shape[0] // 2
    levels = [*range(chips // 2, chips), *reversed(range(chips // 2))]
    order = [2 * level + core for level in levels for core in (1, 0)]
    return lax.all_to_all(value, "dp", split_axis=0, concat_axis=0, tiled=True, axis_index_groups=[order])


def body(grad, momentum, old_slot, new_slot):
    merged, start = merge(grad, momentum, old_slot, new_slot)
    got = exchange(start)
    slots, rows, columns = got.shape
    update, merged = polish(got.reshape(slots * rows, columns), merged, lax.axis_size("mp"))
    update = update.reshape(slots, rows, columns)
    return merged, keep(exchange(update))


def solution(mesh):
    placed = (P(None, "dp", "mp"), P(None, "dp", "mp"), P(), P())
    return jax.shard_map(
        body,
        mesh=mesh,
        in_specs=placed,
        out_specs=(P(None, "dp", "mp"), P(None, "dp", "mp")),
        check_vma=False,
    )
```

```python
import math

import jax
import jax.numpy as jnp
from jax import lax
from jax.experimental import pallas as pl
from jax.experimental.pallas import tpu as pltpu
from jax.sharding import PartitionSpec as P

coef_a = 3.4445
coef_b = -4.775
coef_c = 2.0315
beta = 0.95
epsilon = 1e-07
TILE = 128
bf16 = jnp.bfloat16
f32 = jnp.float32


def merge_kernel(
    old_ref, new_ref, grad_ref, mom_ref, merged_ref, start_ref, old, new, grad, mom, sems
):
    loads = [
        pltpu.make_async_copy(source, target, sems.at[at])
        for at, (source, target) in enumerate(
            [(mom_ref, mom), (grad_ref, grad), (old_ref, old), (new_ref, new)]
        )
    ]
    for load in loads:
        load.start()
    for load in loads:
        load.wait()
    for j in range(grad.shape[0]):
        slot = new[j]
        value = beta * mom[old[j]] + grad[slot].astype(f32)
        start_ref[slot] = value.astype(bf16)
        merged_ref[slot] = value


def merge(grad, momentum, old_slot, new_slot):
    hbm = pl.BlockSpec(memory_space=pltpu.HBM)
    return pl.pallas_call(
        merge_kernel,
        out_shape=(
            jax.ShapeDtypeStruct(momentum.shape, f32),
            jax.ShapeDtypeStruct(grad.shape, bf16),
        ),
        in_specs=[hbm] * 4,
        out_specs=(pl.BlockSpec(memory_space=pltpu.VMEM),) * 2,
        scratch_shapes=[
            pltpu.SMEM(old_slot.shape, jnp.int32),
            pltpu.SMEM(new_slot.shape, jnp.int32),
            pltpu.VMEM(grad.shape, bf16),
            pltpu.VMEM(momentum.shape, f32),
            pltpu.SemaphoreType.DMA((4,)),
        ],
        compiler_params=pltpu.CompilerParams(vmem_limit_bytes=32 << 20),
    )(*(pltpu.with_memory_space_constraint(x, pltpu.HBM) for x in (old_slot, new_slot, grad, momentum)))


def upper(count):
    return [(r, s) for r in range(count) for s in range(r, count)]


def exponent(bound):
    return jnp.floor(jnp.log(jnp.maximum(bound, 1e-30)) * (1.0 / math.log(2.0))) - 14.0


def power(value):
    return jnp.exp(value * math.log(2.0))


def spot(rows):
    row = lax.broadcasted_iota(jnp.int32, (rows, TILE), 0)
    return (row % 8 == 7) & (lax.broadcasted_iota(jnp.int32, (rows, TILE), 1) == 0)


def gram_kernel(x_ref, out_ref):
    x = x_ref[...]
    half = x.shape[0] // 2
    split = half // TILE
    dots = lambda p, q: lax.dot_general(p, q, (((1,), (1,)), ((), ())), preferred_element_type=f32)
    top, corner = dots(x[:half], x), dots(x[half:], x[half:])
    wide = x.astype(f32)
    bound = jnp.max(jnp.sum(wide * wide, axis=1, keepdims=True), axis=0, keepdims=True)
    power_of = exponent(bound)
    scale = power(-power_of)
    parts = out_ref.shape[0]
    for at, (r, s) in enumerate(upper(x.shape[0] // TILE)):
        gram, r, s = (top, r, s) if r < split else (corner, r - split, s - split)
        block = gram[r * TILE : (r + 1) * TILE, s * TILE : (s + 1) * TILE] * scale
        if at == 0:
            block = jnp.where(spot(TILE), power_of, block)
        out_ref[:, at * 8 : (at + 1) * 8, :] = block.reshape(parts, 8, TILE)


def sum_kernel(parts_ref, out_ref):
    powers = parts_ref[:, 7:8, 0:1]
    power_of = jnp.max(powers, axis=0) + math.ceil(math.log2(parts_ref.shape[0]))
    scales = power(powers - power_of)
    total = jnp.zeros(out_ref.shape, f32)
    for k in range(parts_ref.shape[0]):
        total += parts_ref[k] * scales[k]
    row = lax.broadcasted_iota(jnp.int32, out_ref.shape, 0)
    marks = (row == 7) & (lax.broadcasted_iota(jnp.int32, out_ref.shape, 1) == 0)
    out_ref[...] = jnp.where(marks, power_of, total)


def split(value):
    high = value.astype(bf16)
    return high, (value - high.astype(f32)).astype(bf16)


def dot(left, right):
    return jnp.dot(left, right, preferred_element_type=f32)


def product(left, right):
    (lh, ll), (rh, rl) = left, right
    return dot(jnp.concatenate([lh, ll, lh], axis=1), jnp.concatenate([rh, rh, rl], axis=0))


def symmetric(left, right):
    half = left[0].shape[0] // 2
    top = product([p[:half] for p in left], right)
    corner = product([p[half:] for p in left], [p[:, half:] for p in right])
    return jnp.concatenate([top, jnp.concatenate([top[:, half:].T, corner], axis=1)], axis=0)


def polish_kernel(width, packed_ref, x_ref, merged_ref, out_ref, kept_ref, gram_ref, done):
    store = pltpu.make_async_copy(merged_ref, kept_ref, done)
    store.start()
    rows = x_ref.shape[0]
    parts = packed_ref.shape[0]
    scale = power(packed_ref[:, 7:8, 0:1])
    row = lax.broadcasted_iota(jnp.int32, (TILE, TILE), 0)
    column = lax.broadcasted_iota(jnp.int32, (TILE, TILE), 1)
    pieces = [(at, r * TILE, s * TILE) for at, (r, s) in enumerate(upper(rows // TILE))]
    load = lambda at, factor: (packed_ref[:, at * 8 : (at + 1) * 8, :] * factor).reshape(TILE, TILE)
    traces = [jnp.where(row == column, load(at, scale), 0.0) for at, r, s in pieces if r == s]
    total = jnp.sum(sum(traces), keepdims=True)
    inverse = 1.0 / (jnp.sqrt(total) + epsilon)
    factor = scale * (inverse * inverse).reshape(1, 1, 1)
    for at, r, s in pieces:
        block = load(at, factor)
        if r == s:
            block = jnp.where(row > column, block.T, block)
        gram_ref[r : r + TILE, s : s + TILE] = block
        if r != s:
            gram_ref[s : s + TILE, r : r + TILE] = block.T
    gram = gram_ref[...]
    row = lax.broadcasted_iota(jnp.int32, (rows, rows), 0)
    diagonal = row == lax.broadcasted_iota(jnp.int32, (rows, rows), 1)
    rests, steps = [], []
    for step in range(3):
        g = split(gram)
        rest = coef_b * gram + coef_c * symmetric(g, g)
        q = split(rest)
        rests.append(rest)
        steps.append(q)
        if step < 2:
            half = coef_a * gram + symmetric(g, q)
        if step == 1:
            both = coef_a * (rests[0] + rests[1]) + symmetric(q, steps[0])
            both += jnp.where(diagonal, coef_a * coef_a, 0.0)
        if step < 2:
            gram = coef_a * half + symmetric(split(half), q)
    whole = split(coef_a * both + symmetric(steps[2], split(both)))
    x = x_ref[...]
    current = dot(whole[0], x) + dot(whole[1], x)
    out_ref[...] = (0.2 * math.sqrt(width) * inverse * current).astype(bf16)
    store.wait()


def keep_kernel(in_ref, out_ref, done):
    copy = pltpu.make_async_copy(in_ref, out_ref, done)
    copy.start()
    copy.wait()


def keep(value):
    return pl.pallas_call(
        keep_kernel,
        out_shape=jax.ShapeDtypeStruct(value.shape, value.dtype),
        in_specs=[pl.BlockSpec(memory_space=pl.ANY)],
        out_specs=pl.BlockSpec(memory_space=pltpu.HBM),
        scratch_shapes=[pltpu.SemaphoreType.DMA],
        compiler_params=pltpu.CompilerParams(vmem_limit_bytes=16 << 20),
    )(value)


def share_out(value):
    side = math.isqrt(value.shape[0])
    turn = [(at + side // 2) % side for at in range(side)]
    order = [side * y + x for y in turn for x in turn]
    return lax.all_to_all(value, "mp", split_axis=0, concat_axis=0, tiled=True, axis_index_groups=[order])


def polish(start, merged, parts):
    rows, columns = start.shape
    vmem = pl.BlockSpec(memory_space=pltpu.VMEM)
    params = pltpu.CompilerParams(vmem_limit_bytes=48 << 20)
    share = (len(upper(rows // TILE)) * 8, TILE)
    packed = pl.pallas_call(
        gram_kernel,
        out_shape=jax.ShapeDtypeStruct((parts, *share), f32),
        in_specs=[vmem],
        out_specs=vmem,
        compiler_params=params,
    )(start)
    packed = packed.astype(jnp.float16)
    packed = share_out(packed)
    total = pl.pallas_call(
        sum_kernel,
        out_shape=jax.ShapeDtypeStruct(share, f32),
        in_specs=[vmem],
        out_specs=vmem,
        compiler_params=params,
    )(packed.astype(f32))
    copies = jnp.broadcast_to(total.astype(jnp.float16), (parts, *share))
    copies = share_out(copies)
    return pl.pallas_call(
        lambda *refs: polish_kernel(columns * parts, *refs),
        out_shape=(
            jax.ShapeDtypeStruct(start.shape, bf16),
            jax.ShapeDtypeStruct(merged.shape, f32),
        ),
        in_specs=[vmem] * 3,
        out_specs=(vmem, pl.BlockSpec(memory_space=pltpu.HBM)),
        scratch_shapes=[pltpu.VMEM((rows, rows), f32), pltpu.SemaphoreType.DMA],
        compiler_params=params,
    )(copies.astype(f32), start, merged)


def exchange(value):
    chips = value.shape[0] // 2
    levels = [(level + 11 * chips // 16) % chips for level in range(chips)]
    order = [2 * level + core for level in levels for core in (1, 0)]
    return lax.all_to_all(value, "dp", split_axis=0, concat_axis=0, tiled=True, axis_index_groups=[order])


def body(grad, momentum, old_slot, new_slot):
    merged, start = merge(grad, momentum, old_slot, new_slot)
    got = exchange(start)
    slots, rows, columns = got.shape
    update, merged = polish(got.reshape(slots * rows, columns), merged, lax.axis_size("mp"))
    update = update.reshape(slots, rows, columns)
    return merged, keep(exchange(update))


def solution(mesh):
    placed = (P(None, "dp", "mp"), P(None, "dp", "mp"), P(), P())
    return jax.shard_map(
        body,
        mesh=mesh,
        in_specs=placed,
        out_specs=(P(None, "dp", "mp"), P(None, "dp", "mp")),
        check_vma=False,
    )
```
